32 devices in a mesh: replica: 8 (over z, x), shard: 4 (over y, core).
Axes of the slice: x: 2, y: 2, z: 4, core: 2. Of those that a mesh axis runs over, the one named last changes fastest.
Arguments:
- images: bfloat16 [96, 197, 384], P(('replica', 'shard')), may hold values from -6 to 6
- counts: int32 [32], P(('replica', 'shard')), may hold values from 1 to 3, 51 in all
- first_gain: bfloat16 [384], P('shard'), may hold values from 0.25 to 1.75
- first_shift: bfloat16 [384], P('shard'), may hold values from -3 to 3
- project_in: bfloat16 [384, 1152], P('shard'), may hold values from -0.4375 to 0.4375
- query_bias: bfloat16 [384], P('shard'), may hold values from -3 to 3
- value_bias: bfloat16 [384], P('shard'), may hold values from -3 to 3
- project_out: bfloat16 [384, 384], P('shard'), may hold values from -0.875 to 0.875
- output_bias: bfloat16 [384], P('shard'), may hold values from -3 to 3
- second_gain: bfloat16 [384], P('shard'), may hold values from 0.25 to 1.75
- second_shift: bfloat16 [384], P('shard'), may hold values from -3 to 3
- expand_weight: bfloat16 [384, 1536], P('shard'), may hold values from -0.3125 to 0.3125
- expand_bias: bfloat16 [1536], P('shard'), may hold values from -3 to 3
- reduce_weight: bfloat16 [1536, 384], P('shard'), may hold values from -0.21875 to 0.21875
- reduce_bias: bfloat16 [384], P('shard'), may hold values from -3 to 3
- cotangent: bfloat16 [96, 197, 384], P(('replica', 'shard')), may hold values from -6 to 6
Outputs:
- output: bfloat16 [96, 197, 384], P(('replica', 'shard'))
- input_grad: bfloat16 [96, 197, 384], P(('replica', 'shard'))
- first_gain_grad: float32 [384], P('shard')
- first_shift_grad: float32 [384], P('shard')
- project_in_grad: float32 [384, 1152], P('shard')
- query_bias_grad: float32 [384], P('shard')
- value_bias_grad: float32 [384], P('shard')
- project_out_grad: float32 [384, 384], P('shard')
- output_bias_grad: float32 [384], P('shard')
- second_gain_grad: float32 [384], P('shard')
- second_shift_grad: float32 [384], P('shard')
- expand_weight_grad: float32 [384, 1536], P('shard')
- expand_bias_grad: float32 [1536], P('shard')
- reduce_weight_grad: float32 [1536, 384], P('shard')
- reduce_bias_grad: float32 [384], P('shard')
The draws below stay inside these ranges and needn't reach their ends.
Inputs may be any that keep to these rules, and one draw needn't show every extreme that they name: Device d holds counts[d] real images in its first slots; the counts sum to 51 and some device's count is 3.
All inputs are finite; a program needn't handle non-finite values.
Results may differ from the reference program's by a relative error of at most 0.012.
The reference program's roundings to bfloat16 on the way count: a program that leaves them out, or rounds other values in their place, can miss the bound.
Values may be sent and summed in bfloat16 or wider, within the bound.
A program may use at most 128 MiB of HBM per device.

```python
import math
import jax
import jax.numpy as jnp
import numpy as np
from jax import lax

D = 384
FF = 1536
HEADS = 6
HEAD_DIM = 64
SEQ = 197
IMG_SLOTS = 3
SLOTS_ALL = 96
IMAGES = 51
DEVICES = 32


def shard_levels(rng, shape, cuts, low, high):
    loudness = 1.0
    for position, shards_of in cuts:
        heights = jax.random.uniform(jax.random.fold_in(jax.random.fold_in(rng, 6), position), (shards_of,), jnp.float32, low / len(cuts), high / len(cuts))
        loudness = loudness * jnp.repeat(jnp.exp(heights), shape[position] // shards_of).reshape((-1,) + (1,) * (len(shape) - 1 - position))
    return loudness


def profile(count, total, bound, lean):
    loads = [(1 << 20) // math.isqrt(rank ** lean) + 1 for rank in range(2, count + 1)]
    surplus, given = total - bound - (count - 1), [1] * (count - 1)
    while surplus > 0:
        free = [i for i in range(count - 1) if given[i] < bound]
        pool, remaining = sum([loads[i] for i in free]), surplus
        for i in free:
            addition = min(bound - given[i], max(1, remaining * loads[i] // pool), surplus)
            given[i] = given[i] + addition
            surplus = surplus - addition
    return np.array([bound] + given)


def ragged_sizes(key, amount, total, limit, skew):
    if amount == 2:
        one = jax.random.randint(key, (), max(1, total - limit), min(limit, total - 1) + 1)
        return jnp.stack([one, total - one])
    lengths = jnp.asarray(profile(amount, total, limit, skew), jnp.int32)
    pairs = (amount - 1) // 2
    donor, receiver = lengths[1:1 + 2 * pairs:2], lengths[2:2 + 2 * pairs:2]
    room = jnp.minimum(donor - 1, limit - receiver)
    shifted = jax.random.randint(jax.random.fold_in(key, 1), (pairs,), 0, 1 << 20) % (room + 1)
    lengths = lengths.at[1:1 + 2 * pairs:2].set(donor - shifted).at[2:2 + 2 * pairs:2].set(receiver + shifted)
    return lengths[jax.random.permutation(jax.random.fold_in(key, 2), amount)]


def gaussian(key, dims, deviation, bound, pieces=(), held_as=jnp.bfloat16):
    entries = jax.random.normal(key, dims, jnp.float32) * deviation
    if len(pieces) > 0:
        entries = shard_levels(key, dims, pieces, -0.22, 0.18) * entries
    return jnp.clip(entries, min=-bound, max=bound).astype(held_as)


def setup_inputs(seed: int = 0) -> dict:
    streams_of = jax.random.split(jax.random.key(seed), 17)
    images = gaussian(streams_of[0], (SLOTS_ALL, SEQ, D), 1.0, 6.0, ((0, 32),))
    counts = ragged_sizes(streams_of[1], DEVICES, IMAGES, IMG_SLOTS, 0).astype(jnp.int32)
    first_gain = jnp.clip(1.0 + 0.15 * jax.random.normal(streams_of[2], (D,), jnp.float32), 0.25, 1.75).astype(jnp.bfloat16)
    first_shift = gaussian(streams_of[3], (D,), 0.5, 3.0, ((0, 4),))
    project_in = gaussian(streams_of[4], (D, 3 * D), (D // 2) ** -0.5, 0.4375, ((0, 4),))
    query_bias = gaussian(streams_of[5], (D,), 0.5, 3.0, ((0, 4),))
    value_bias = gaussian(streams_of[6], (D,), 0.5, 3.0, ((0, 4),))
    project_out = gaussian(streams_of[7], (D, D), (D // 8) ** -0.5, 0.875, ((0, 4),))
    output_bias = gaussian(streams_of[8], (D,), 0.5, 3.0, ((0, 4),))
    second_gain = jnp.clip(1.0 + 0.15 * jax.random.normal(streams_of[9], (D,), jnp.float32), 0.25, 1.75).astype(jnp.bfloat16)
    second_shift = gaussian(streams_of[10], (D,), 0.5, 3.0, ((0, 4),))
    expand_weight = gaussian(streams_of[11], (D, FF), D ** -0.5, 0.3125, ((0, 4),))
    expand_bias = gaussian(streams_of[12], (FF,), 0.5, 3.0, ((0, 4),))
    reduce_weight = gaussian(streams_of[13], (FF, D), (FF // 2) ** -0.5, 0.21875, ((0, 4),))
    reduce_bias = gaussian(streams_of[14], (D,), 0.5, 3.0, ((0, 4),))
    cotangent = gaussian(streams_of[15], (SLOTS_ALL, SEQ, D), 1.0, 6.0, ((0, 32),))
    return dict(images=images, counts=counts, first_gain=first_gain, first_shift=first_shift, project_in=project_in, query_bias=query_bias, value_bias=value_bias, project_out=project_out, output_bias=output_bias, second_gain=second_gain, second_shift=second_shift, expand_weight=expand_weight, expand_bias=expand_bias, reduce_weight=reduce_weight, reduce_bias=reduce_bias, cotangent=cotangent)


EPS = 1e-06
HIGHEST = lax.Precision.HIGHEST

@jax.custom_vjp
def low(v):
    return lax.optimization_barrier(v.astype(jnp.bfloat16)).astype(jnp.float32)

@jax.custom_vjp
def low_back(v):
    return v

def low_keep(v):
    return (low(v), None)

def low_pass(kept, grad):
    return (grad,)

def back_keep(v):
    return (v, None)

def back_low(kept, grad):
    return (low(grad),)
low.defvjp(low_keep, low_pass)
low_back.defvjp(back_keep, back_low)

def layer_norm(hidden_rows, gain_vector, shift_vector):
    center = hidden_rows - lax.optimization_barrier(jnp.mean(hidden_rows, -1, keepdims=True))
    spread = lax.optimization_barrier(jnp.mean(center * center, -1, keepdims=True))
    return center * lax.rsqrt(spread + EPS) * gain_vector + shift_vector

def matmul(left, right):
    return jnp.dot(left, right, precision=HIGHEST, preferred_element_type=jnp.float32)

def forward(images_block, params, alive_mask):
    first_gain, first_shift, project_in, query_bias, value_bias, project_out, output_bias, second_gain, second_shift, expand_weight, expand_bias, reduce_weight, reduce_bias = params
    image_count, length, feature_width = images_block.shape
    tokens = images_block.reshape(-1, feature_width)
    normed_one = low(layer_norm(tokens, first_gain, first_shift))
    triple = matmul(normed_one, project_in)
    head_shape = (image_count, length, HEADS, HEAD_DIM)
    queries = low_back(low(triple[:, :feature_width] + query_bias)).reshape(head_shape)
    key_rows = low_back(low(triple[:, feature_width:2 * feature_width])).reshape(head_shape)
    value_rows = low_back(low(triple[:, 2 * feature_width:] + value_bias)).reshape(head_shape)
    scores = low_back(jnp.einsum('sqhd,skhd->shqk', queries, key_rows, precision=HIGHEST) * HEAD_DIM ** (-0.5))
    row_max = lax.optimization_barrier(jnp.max(scores, -1, keepdims=True))
    log_total = row_max + jnp.log(lax.optimization_barrier(jnp.sum(jnp.exp(scores - row_max), -1, keepdims=True)))
    attend_weights = low(jnp.exp(scores - log_total))
    mixed = jnp.einsum('shqk,skhd->sqhd', attend_weights, value_rows, precision=HIGHEST)
    mixed = low_back(low(mixed.reshape(-1, feature_width)))
    middle = tokens + low_back(matmul(mixed, project_out) + output_bias)
    normed_two = low(layer_norm(middle, second_gain, second_shift))
    before_gelu = low_back(matmul(normed_two, expand_weight) + expand_bias)
    hidden = low(jax.nn.gelu(before_gelu, approximate=False))
    result = middle + low_back(matmul(hidden, reduce_weight) + reduce_bias)
    return result.reshape(image_count, length, feature_width) * alive_mask[:, None, None]

def reference(images, counts, first_gain, first_shift, project_in, query_bias, value_bias, project_out, output_bias, second_gain, second_shift, expand_weight, expand_bias, reduce_weight, reduce_bias, cotangent):
    params = tuple((item.astype(jnp.float32) for item in (first_gain, first_shift, project_in, query_bias, value_bias, project_out, output_bias, second_gain, second_shift, expand_weight, expand_bias, reduce_weight, reduce_bias)))
    slot_index = jnp.arange(SLOTS_ALL).astype(jnp.int32)
    alive = (slot_index % IMG_SLOTS < counts[slot_index // IMG_SLOTS]).astype(jnp.float32)
    group_size = IMG_SLOTS * 8
    image_blocks = images.astype(jnp.float32).reshape(-1, group_size, SEQ, D)
    grad_blocks = cotangent.astype(jnp.float32).reshape(-1, group_size, SEQ, D)
    alive_blocks = alive.reshape(-1, group_size)

    def scan_step(running, block_items):
        image_part, grad_part, alive_part = block_items
        result, pullback = jax.vjp(lambda inputs, weights: forward(inputs, weights, alive_part), image_part, params)
        input_part, weight_part = pullback(grad_part)
        running = jax.tree.map(lambda total, term: total + term, running, weight_part)
        return (running, (result.astype(jnp.bfloat16), input_part.astype(jnp.bfloat16)))
    zeros = jax.tree.map(lambda item: jnp.zeros(item.shape, jnp.float32), params)
    gradients, (outputs, input_grads) = lax.scan(scan_step, zeros, (image_blocks, grad_blocks, alive_blocks))
    output = outputs.reshape(SLOTS_ALL, SEQ, D)
    input_grad = input_grads.reshape(SLOTS_ALL, SEQ, D)
    return (output, input_grad, gradients[0], gradients[1], gradients[2], gradients[3], gradients[4], gradients[5], gradients[6], gradients[7], gradients[8], gradients[9], gradients[10], gradients[11], gradients[12])
```

```python
import jax
import jax.numpy as jnp
from jax import lax
from jax.experimental import pallas as pl
from jax.experimental.pallas import tpu as pltpu
from jax.sharding import PartitionSpec as P

HEADS = 6
HEAD_DIM = 64


EPS = 1e-06


def layer_norm(hidden_rows, gain_vector, shift_vector):
    center = hidden_rows - jnp.mean(hidden_rows, -1, keepdims=True)
    spread = jnp.mean(center * center, -1, keepdims=True)
    return center * lax.rsqrt(spread + EPS) * gain_vector + shift_vector


def gelu_exact(argument):
    return jax.nn.gelu(argument, approximate=False)


def column_total(gradient):
    return jnp.sum(gradient.astype(jnp.float32), axis=0)


def outer_sum(left, right):
    return lax.dot_general(
        left, right, (((0,), (0,)), ((), ())), preferred_element_type=jnp.float32
    )


def back_product(gradient, weight):
    return lax.dot_general(
        gradient, weight, (((1,), (1,)), ((), ())), preferred_element_type=jnp.float32
    )


def attend_scores(queries, key_rows, score_scale):
    return (
        jnp.einsum("sqhd,skhd->shqk", queries, key_rows, preferred_element_type=jnp.float32)
        * score_scale
    )


def body(
    images,
    counts,
    first_gain,
    first_shift,
    project_in,
    query_bias,
    value_bias,
    project_out,
    output_bias,
    second_gain,
    second_shift,
    expand_weight,
    expand_bias,
    reduce_weight,
    reduce_bias,
    cotangent,
):
    slot_count, length, feature_width = images.shape
    score_scale = HEAD_DIM ** (-0.5)
    head_shape = (slot_count, length, HEADS, HEAD_DIM)
    gathered = (
        lax.all_gather(first_gain, "shard", axis=0, tiled=True),
        lax.all_gather(first_shift, "shard", axis=0, tiled=True),
        lax.all_gather(project_in, "shard", axis=0, tiled=True),
        lax.all_gather(query_bias, "shard", axis=0, tiled=True),
        lax.all_gather(value_bias, "shard", axis=0, tiled=True),
        lax.all_gather(project_out, "shard", axis=0, tiled=True),
        lax.all_gather(output_bias, "shard", axis=0, tiled=True),
        lax.all_gather(second_gain, "shard", axis=0, tiled=True),
        lax.all_gather(second_shift, "shard", axis=0, tiled=True),
        lax.all_gather(expand_weight, "shard", axis=0, tiled=True),
        lax.all_gather(expand_bias, "shard", axis=0, tiled=True),
        lax.all_gather(reduce_weight, "shard", axis=0, tiled=True),
        lax.all_gather(reduce_bias, "shard", axis=0, tiled=True),
    )
    (
        gain_one,
        shift_one,
        inproj_full,
        query_shift,
        value_shift,
        outproj_full,
        out_shift,
        gain_two,
        shift_two,
        expand_full,
        expand_shift,
        reduce_full,
        reduce_shift,
    ) = gathered
    gain_one = gain_one.astype(jnp.float32)
    gain_two = gain_two.astype(jnp.float32)
    alive = (jnp.arange(slot_count) < counts[0]).astype(jnp.float32)
    tokens = images.astype(jnp.float32).reshape(-1, feature_width)
    normed_one = layer_norm(tokens, gain_one, shift_one.astype(jnp.float32)).astype(jnp.bfloat16)
    triple = jnp.dot(normed_one, inproj_full, preferred_element_type=jnp.float32)
    queries = (
        (triple[:, :feature_width] + query_shift.astype(jnp.float32))
        .astype(jnp.bfloat16)
        .reshape(head_shape)
    )
    key_rows = triple[:, feature_width : 2 * feature_width].astype(jnp.bfloat16).reshape(head_shape)
    value_rows = (
        (triple[:, 2 * feature_width :] + value_shift.astype(jnp.float32))
        .astype(jnp.bfloat16)
        .reshape(head_shape)
    )
    scores = attend_scores(queries, key_rows, score_scale)
    row_max = jnp.max(scores, -1, keepdims=True)
    log_total = row_max + jnp.log(jnp.sum(jnp.exp(scores - row_max), -1, keepdims=True))
    attend_weights = jnp.exp(scores - log_total).astype(jnp.bfloat16)
    mixed = jnp.einsum(
        "shqk,skhd->sqhd", attend_weights, value_rows, preferred_element_type=jnp.float32
    )
    mixed = mixed.reshape(-1, feature_width).astype(jnp.bfloat16)
    middle = (
        tokens
        + jnp.dot(mixed, outproj_full, preferred_element_type=jnp.float32)
        + out_shift.astype(jnp.float32)
    )
    normed_two = layer_norm(middle, gain_two, shift_two.astype(jnp.float32)).astype(jnp.bfloat16)
    before_gelu = jnp.dot(
        normed_two, expand_full, preferred_element_type=jnp.float32
    ) + expand_shift.astype(jnp.float32)
    hidden = gelu_exact(before_gelu).astype(jnp.bfloat16)
    result = (
        middle
        + jnp.dot(hidden, reduce_full, preferred_element_type=jnp.float32)
        + reduce_shift.astype(jnp.float32)
    )
    output = (result.reshape(slot_count, length, feature_width) * alive[:, None, None]).astype(
        jnp.bfloat16
    )
    reduce_back, expand_back, gain_two_back, outproj_back, inproj_back, gain_one_back = (
        lax.all_gather(reduce_weight, "shard", axis=0, tiled=True),
        lax.all_gather(expand_weight, "shard", axis=0, tiled=True),
        lax.all_gather(second_gain, "shard", axis=0, tiled=True),
        lax.all_gather(project_out, "shard", axis=0, tiled=True),
        lax.all_gather(project_in, "shard", axis=0, tiled=True),
        lax.all_gather(first_gain, "shard", axis=0, tiled=True),
    )
    gain_two_back = gain_two_back.astype(jnp.float32)
    gain_one_back = gain_one_back.astype(jnp.float32)
    out_grad = (cotangent.astype(jnp.float32) * alive[:, None, None]).reshape(-1, feature_width)
    branch_grad = out_grad.astype(jnp.bfloat16)
    reduce_weight_grad = outer_sum(hidden, branch_grad)
    reduce_bias_grad = column_total(branch_grad)
    hidden_grad = back_product(branch_grad, reduce_back)
    _, gelu_pull = jax.vjp(gelu_exact, before_gelu)
    expand_grad = gelu_pull(hidden_grad)[0].astype(jnp.bfloat16)
    expand_weight_grad = outer_sum(normed_two, expand_grad)
    expand_bias_grad = column_total(expand_grad)
    normed_two_grad = back_product(expand_grad, expand_back)
    _, norm_two_pull = jax.vjp(layer_norm, middle, gain_two_back, jnp.zeros_like(gain_two_back))
    middle_norm_grad, second_gain_grad, second_shift_grad = norm_two_pull(normed_two_grad)
    middle_grad = out_grad + middle_norm_grad
    proj_grad = middle_grad.astype(jnp.bfloat16)
    project_out_grad = outer_sum(mixed, proj_grad)
    output_bias_grad = column_total(proj_grad)
    mixed_grad = back_product(proj_grad, outproj_back).astype(jnp.bfloat16).reshape(head_shape)
    scores_again = attend_scores(queries, key_rows, score_scale)
    probs_exact = jnp.exp(scores_again - log_total)
    probs_round = probs_exact.astype(jnp.bfloat16)
    values_grad = jnp.einsum(
        "shqk,sqhd->skhd", probs_round, mixed_grad, preferred_element_type=jnp.float32
    )
    probs_grad = jnp.einsum(
        "sqhd,skhd->shqk", mixed_grad, value_rows, preferred_element_type=jnp.float32
    )
    scores_grad = probs_exact * (probs_grad - jnp.sum(probs_exact * probs_grad, -1, keepdims=True))
    scores_grad = scores_grad.astype(jnp.bfloat16)
    queries_grad = (
        jnp.einsum("shqk,skhd->sqhd", scores_grad, key_rows, preferred_element_type=jnp.float32)
        * score_scale
    )
    keys_grad = (
        jnp.einsum("shqk,sqhd->skhd", scores_grad, queries, preferred_element_type=jnp.float32)
        * score_scale
    )
    triple_grad = jnp.concatenate(
        (
            queries_grad.reshape(-1, feature_width),
            keys_grad.reshape(-1, feature_width),
            values_grad.reshape(-1, feature_width),
        ),
        axis=1,
    ).astype(jnp.bfloat16)
    project_in_grad = outer_sum(normed_one, triple_grad)
    query_bias_grad = column_total(triple_grad[:, :feature_width])
    value_bias_grad = column_total(triple_grad[:, 2 * feature_width :])
    normed_one_grad = back_product(triple_grad, inproj_back)
    _, norm_one_pull = jax.vjp(layer_norm, tokens, gain_one_back, jnp.zeros_like(gain_one_back))
    tokens_norm_grad, first_gain_grad, first_shift_grad = norm_one_pull(normed_one_grad)
    input_grad = (
        (middle_grad + tokens_norm_grad)
        .reshape(slot_count, length, feature_width)
        .astype(jnp.bfloat16)
    )
    shares = (
        lax.psum_scatter(first_gain_grad, "shard", scatter_dimension=0, tiled=True),
        lax.psum_scatter(first_shift_grad, "shard", scatter_dimension=0, tiled=True),
        lax.psum_scatter(project_in_grad, "shard", scatter_dimension=0, tiled=True),
        lax.psum_scatter(query_bias_grad, "shard", scatter_dimension=0, tiled=True),
        lax.psum_scatter(value_bias_grad, "shard", scatter_dimension=0, tiled=True),
        lax.psum_scatter(project_out_grad, "shard", scatter_dimension=0, tiled=True),
        lax.psum_scatter(output_bias_grad, "shard", scatter_dimension=0, tiled=True),
        lax.psum_scatter(second_gain_grad, "shard", scatter_dimension=0, tiled=True),
        lax.psum_scatter(second_shift_grad, "shard", scatter_dimension=0, tiled=True),
        lax.psum_scatter(expand_weight_grad, "shard", scatter_dimension=0, tiled=True),
        lax.psum_scatter(expand_bias_grad, "shard", scatter_dimension=0, tiled=True),
        lax.psum_scatter(reduce_weight_grad, "shard", scatter_dimension=0, tiled=True),
        lax.psum_scatter(reduce_bias_grad, "shard", scatter_dimension=0, tiled=True),
    )
    totals = tuple(
        lax.psum(
            (
                shares[0],
                shares[1],
                shares[2],
                shares[3],
                shares[4],
                shares[5],
                shares[6],
                shares[7],
                shares[8],
                shares[9],
                shares[10],
                shares[11],
                shares[12],
            ),
            "replica",
        )
    )
    return (
        output,
        input_grad,
        totals[0],
        totals[1],
        totals[2],
        totals[3],
        totals[4],
        totals[5],
        totals[6],
        totals[7],
        totals[8],
        totals[9],
        totals[10],
        totals[11],
        totals[12],
    )


ROWS = 208
MESH = pl.DeviceIdType.MESH


def mm(left, right):
    return jnp.dot(left, right, preferred_element_type=jnp.float32)


def mega(
    images_ref, alive_ref, cot_ref, pack_ref, win_ref, wout_ref, wexp_ref, wred_ref,
    out_ref, ingrad_ref, gin_ref, gout_ref, gexp_ref, gred_ref, gvec_ref,
    WI, WO, WE, WR, VG, VEC, BE,
    A1, QKV, PR, MIX, H1, XH1, XH2, RS1, RS2, A2, HID, GP, DM, DU, DH1, DZ, DMX, DT,
    GB, AR, BS, BR, CS, CR, DR, FIN, ACC, VS, VR,
    gss, grs, rss, rrs,
):
    D = 384
    slots, length, _ = images_ref.shape
    replica, shard = lax.axis_index("replica"), lax.axis_index("shard")
    z, x = replica // 2, replica % 2
    y, c = shard // 2, shard % 2
    sib = (replica, y * 2 + 1 - c)
    ypart = (replica, (1 - y) * 2 + c)
    xpart = (z * 2 + 1 - x, shard)
    zparts = [(((z + d) % 4) * 2 + x, shard) for d in (1, 2, 3)]

    barrier = pltpu.get_barrier_semaphore()
    for who in [sib, ypart, xpart] + zparts:
        pl.semaphore_signal(barrier, inc=1, device_id=who, device_id_type=MESH)
    pl.semaphore_wait(barrier, 6)

    def remote(src, dst, ss, rs, who):
        return pltpu.make_async_remote_copy(
            src_ref=src, dst_ref=dst, send_sem=ss, recv_sem=rs, device_id=who, device_id_type=MESH
        )

    items = [(pack_ref, VG, 16), (win_ref, WI, 96), (wout_ref, WO, 96), (wexp_ref, WE, 96), (wred_ref, WR, 384)]
    other_y = (1 - y) * 2 + c
    to_y, to_sib, forward = [], [], []
    for k, (src, full, rows) in enumerate(items):
        mine = full.at[pl.ds(pl.multiple_of(shard * rows, 16), rows)]
        theirs = full.at[pl.ds(pl.multiple_of(other_y * rows, 16), rows)]
        to_y.append(remote(src, mine, gss.at[0, k], grs.at[0, k], ypart))
        to_sib.append(remote(src, mine, gss.at[1, k], grs.at[1, k], sib))
        forward.append(remote(theirs, theirs, gss.at[2, k], grs.at[2, k], sib))
    for k in range(5):
        to_y[k].start()
    for k in range(5):
        to_sib[k].start()
    for src, full, rows in items:
        full[pl.ds(pl.multiple_of(shard * rows, 16), rows), :] = src[...]

    def arrived(ks):
        for k in ks:
            to_y[k].wait_recv()
            forward[k].start()
        for k in ks:
            to_sib[k].wait_recv()
            forward[k].wait_recv()

    arrived([0, 1])
    lane = lax.broadcasted_iota(jnp.int32, (128, D), 1)
    sub = lax.broadcasted_iota(jnp.int32, (128, D), 0)
    place = [jnp.where((lane == sub + 96 * s) & (sub < 96), 1.0, 0.0).astype(jnp.bfloat16) for s in range(4)]
    blocks = [VG[16 * s : 16 * s + 16, :] for s in range(4)]
    VEC[...] = sum(mm(blocks[s], place[s]) for s in range(4))
    for s in range(4):
        BE[s : s + 1, :] = sum(mm(blocks[s], place[k])[8 + k : 9 + k, :] for k in range(4))
    row = lambda j: VEC[j : j + 1, :]
    half = lax.broadcasted_iota(jnp.int32, (ROWS, 128), 1) < 64
    keep = lax.broadcasted_iota(jnp.int32, (ROWS, ROWS), 1) < length
    scale = HEAD_DIM ** (-0.5)
    pairs = HEADS // 2

    def at(i):
        return pl.ds(pl.multiple_of(i * ROWS, 16), ROWS)

    def pad(value):
        return jnp.concatenate([value, jnp.zeros((ROWS - length, D), value.dtype)], axis=0)

    def norm(value):
        center = value - jnp.mean(value, -1, keepdims=True)
        inverse = lax.rsqrt(jnp.mean(center * center, -1, keepdims=True) + EPS)
        return center * inverse, inverse

    def norm_back(grad, gain, unit, inverse):
        g = grad * gain
        return inverse * (g - jnp.mean(g, -1, keepdims=True) - unit * jnp.mean(g * unit, -1, keepdims=True))

    def pick(h, value):
        zero = jnp.zeros_like(value)
        return jnp.where(half, value, zero) if h == 0 else jnp.where(half, zero, value)

    def nt(left, right):
        return lax.dot_general(left, right, (((1,), (1,)), ((), ())), preferred_element_type=jnp.float32)

    def tn(left, right):
        return lax.dot_general(left, right, (((0,), (0,)), ((), ())), preferred_element_type=jnp.float32)

    @pl.loop(0, slots)
    def _(i):
        r = at(i)
        tokens = pad(images_ref[i].astype(jnp.float32))
        unit, inverse = norm(tokens)
        H1[r, :] = tokens
        XH1[r, :] = unit
        RS1[r, :] = jnp.broadcast_to(inverse, (ROWS, 128))
        A1[r, :] = (unit * row(0) + row(1)).astype(jnp.bfloat16)
        a1 = A1[r, :]
        QKV[r, 0:D] = (mm(a1, WI[:, 0:D]) + row(2)).astype(jnp.bfloat16)
        QKV[r, D : 2 * D] = mm(a1, WI[:, D : 2 * D]).astype(jnp.bfloat16)
        QKV[r, 2 * D : 3 * D] = (mm(a1, WI[:, 2 * D : 3 * D]) + row(3)).astype(jnp.bfloat16)
        for p in range(pairs):
            q = QKV[r, p * 128 : p * 128 + 128]
            k = QKV[r, D + p * 128 : D + p * 128 + 128]
            v = QKV[r, 2 * D + p * 128 : 2 * D + p * 128 + 128]
            both = []
            for h in range(2):
                scores = jnp.where(keep, nt(pick(h, q), k) * scale, -1e30)
                e = jnp.exp(scores - jnp.max(scores, -1, keepdims=True))
                prob = e * (1.0 / jnp.sum(e, -1, keepdims=True))
                PR[i * HEADS + p * 2 + h] = prob
                both.append(mm(prob.astype(jnp.bfloat16), v))
            MIX[r, p * 128 : p * 128 + 128] = jnp.where(half, both[0], both[1]).astype(jnp.bfloat16)

    arrived([2, 3])

    @pl.loop(0, slots)
    def _(i):
        r = at(i)
        middle = H1[r, :] + mm(MIX[r, :], WO[...]) + row(4)
        H1[r, :] = middle
        unit, inverse = norm(middle)
        XH2[r, :] = unit
        RS2[r, :] = jnp.broadcast_to(inverse, (ROWS, 128))
        A2[r, :] = (unit * row(5) + row(6)).astype(jnp.bfloat16)
        a2 = A2[r, :]
        for s in range(4):
            cols = slice(s * D, s * D + D)
            u = mm(a2, WE[:, cols]) + BE[s : s + 1, :]
            cdf = 0.5 * (1.0 + lax.erf(u * (0.5**0.5)))
            HID[r, cols] = (u * cdf).astype(jnp.bfloat16)
            GP[r, cols] = cdf + u * (jnp.exp(-0.5 * u * u) * 0.3989422804014327)
        DM[r, :] = pad(cot_ref[i].astype(jnp.float32) * alive_ref[i]).astype(jnp.bfloat16)

    arrived([4])
    VS[...] = jnp.zeros_like(VS)

    def tally(j, value):
        VS[0, j : j + 1, :] += jnp.sum(value, axis=0, keepdims=True)

    @pl.loop(0, slots)
    def _(i):
        r = at(i)
        result = H1[r, :] + mm(HID[r, :], WR[...]) + row(7)
        out_ref[i] = (result * alive_ref[i]).astype(jnp.bfloat16)[:length]
        dm = DM[r, :]
        tally(7, dm.astype(jnp.float32))
        for s in range(4):
            cols = slice(s * D, s * D + D)
            du = (nt(dm, WR[cols, :]) * GP[r, cols]).astype(jnp.bfloat16)
            DU[r, cols] = du
            tally(8 + s, du.astype(jnp.float32))

    def step_a(n):
        return remote(GB.at[n, 1 - c], AR.at[n], rss.at[n, 0], rrs.at[n, 0], sib)

    def step_b(n):
        return remote(BS.at[n], BR.at[n], rss.at[n, 1], rrs.at[n, 1], ypart)

    def step_c(n):
        return remote(CS.at[n, pl.ds(pl.multiple_of((1 - x) * 192, 16), 192)], CR.at[n], rss.at[n, 2], rrs.at[n, 2], xpart)

    def steps_d(n):
        return [
            remote(CS.at[n, pl.ds(pl.multiple_of(x * 192 + ((z + d) % 4) * 48, 16), 48)], DR.at[n, d - 1],
                   rss.at[n, 2 + d], rrs.at[n, 2 + d], zparts[d - 1])
            for d in (1, 2, 3)
        ]

    def steps_e(n):
        piece = FIN.at[n, pl.ds(pl.multiple_of(x * 192 + z * 48, 16), 48)]
        return [remote(piece, piece, rss.at[n, 5 + d], rrs.at[n, 5 + d], zparts[d - 1]) for d in (1, 2, 3)]

    def step_f(n):
        piece = FIN.at[n, pl.ds(pl.multiple_of(x * 192, 16), 192)]
        return remote(piece, piece, rss.at[n, 9], rrs.at[n, 9], xpart)

    def do_a(n):
        step_a(n).start()

    def do_b(n):
        step_a(n).wait_recv()
        BS[n] = (GB[n, c, 1 - y].astype(jnp.float32) + AR[n, 1 - y].astype(jnp.float32)).astype(jnp.bfloat16)
        step_b(n).start()
        ACC[n] = GB[n, c, y].astype(jnp.float32) + AR[n, y].astype(jnp.float32)

    def do_c(n):
        step_b(n).wait_recv()
        total = ACC[n] + BR[n].astype(jnp.float32)
        ACC[n] = total
        CS[n] = total.astype(jnp.bfloat16)
        step_c(n).start()

    def do_d(n):
        step_c(n).wait_recv()
        step_c(n).wait_send()
        rows = pl.ds(pl.multiple_of(x * 192, 16), 192)
        total = ACC[n, rows, :] + CR[n].astype(jnp.float32)
        ACC[n, rows, :] = total
        CS[n, rows, :] = total.astype(jnp.bfloat16)
        for copy in steps_d(n):
            copy.start()

    def do_e(n):
        for copy in steps_d(n):
            copy.wait_recv()
        rows = pl.ds(pl.multiple_of(x * 192 + z * 48, 16), 48)
        total = ACC[n, rows, :] + DR[n, 0].astype(jnp.float32) + DR[n, 1].astype(jnp.float32) + DR[n, 2].astype(jnp.float32)
        FIN[n, rows, :] = total.astype(jnp.bfloat16)
        for copy in steps_e(n):
            copy.start()

    def do_f(n):
        for copy in steps_e(n):
            copy.wait_recv()
        step_f(n).start()

    def do_end(n):
        step_f(n).wait_recv()

    def put(n, cols_at, grad):
        rows = grad.shape[0] // 4
        for s in range(4):
            GB[n, s % 2, s // 2, cols_at : cols_at + rows, :] = grad[s * rows : s * rows + rows, :].astype(jnp.bfloat16)

    dm_all = DM[...]
    for s in range(4):
        GB[0, s % 2, s // 2] = tn(HID[:, s * D : s * D + D], dm_all).astype(jnp.bfloat16)
    do_a(0)

    a2_all = A2[...]
    for s in range(4):
        put(1, s * 96, tn(a2_all, DU[:, s * D : s * D + D]))
    do_b(0)
    do_a(1)

    @pl.loop(0, slots)
    def _(i):
        r = at(i)
        da2 = nt(DU[r, :], WE[...])
        unit = XH2[r, :]
        tally(5, da2 * unit)
        tally(6, da2)
        dh1 = DM[r, :].astype(jnp.float32) + norm_back(da2, row(5), unit, RS2[r, 0:1])
        DH1[r, :] = dh1
        dz = dh1.astype(jnp.bfloat16)
        DZ[r, :] = dz
        tally(4, dz.astype(jnp.float32))
        DMX[r, :] = nt(dz, WO[...]).astype(jnp.bfloat16)

    do_b(1)
    put(2, 288, tn(MIX[...], DZ[...]))

    def attend_back(i):
        r = at(i)
        for p in range(pairs):
            cols = slice(p * 128, p * 128 + 128)
            kcols = slice(D + p * 128, D + p * 128 + 128)
            vcols = slice(2 * D + p * 128, 2 * D + p * 128 + 128)
            q, k, v, dmx = QKV[r, cols], QKV[r, kcols], QKV[r, vcols], DMX[r, cols]
            dq, dk, dv = [], 0.0, 0.0
            for h in range(2):
                prob = PR[i * HEADS + p * 2 + h]
                dmh = pick(h, dmx)
                dv = dv + tn(prob.astype(jnp.bfloat16), dmh)
                dp = nt(dmh, v)
                ds = (prob * (dp - jnp.sum(prob * dp, -1, keepdims=True))).astype(jnp.bfloat16)
                dq.append(mm(ds, k))
                dk = dk + tn(ds, pick(h, q))
            dq = (jnp.where(half, dq[0], dq[1]) * scale).astype(jnp.bfloat16)
            DT[r, cols] = dq
            DT[r, kcols] = (dk * scale).astype(jnp.bfloat16)
            DT[r, vcols] = dv.astype(jnp.bfloat16)
        tally(2, DT[r, 0:D].astype(jnp.float32))
        tally(3, DT[r, 2 * D : 3 * D].astype(jnp.float32))

    @pl.loop(0, 1)
    def _(i):
        attend_back(i)

    do_c(0)

    @pl.loop(1, 2)
    def _(i):
        attend_back(i)

    do_d(0)
    do_c(1)

    @pl.loop(2, slots)
    def _(i):
        attend_back(i)

    do_e(0)
    do_d(1)
    a1_all = A1[...]
    for s in range(3):
        put(2, s * 96, tn(a1_all, DT[:, s * D : s * D + D]))
    do_a(2)
    do_f(0)
    do_e(1)

    @pl.loop(0, slots)
    def _(i):
        r = at(i)
        da1 = nt(DT[r, :], WI[...])
        unit = XH1[r, :]
        tally(0, da1 * unit)
        tally(1, da1)
        grad = DH1[r, :] + norm_back(da1, row(0), unit, RS1[r, 0:1])
        ingrad_ref[i] = grad.astype(jnp.bfloat16)[:length]

    zone = ((z + 1 - 2 * (z % 2)) * 2 + x, shard)
    vec_steps = [
        remote(VS.at[k], VR.at[k], rss.at[3, k], rrs.at[3, k], who)
        for k, who in enumerate([sib, ypart, xpart, zone, zparts[1]])
    ]

    def vec(k):
        if k > 0:
            vec_steps[k - 1].wait_recv()
            VS[k] = VS[k - 1] + VR[k - 1]
        if k < 5:
            vec_steps[k].start()

    do_b(2)
    vec(0)
    do_f(1)
    do_end(0)
    gred_ref[...] = FIN[0].astype(jnp.float32)
    vec(1)
    do_c(2)
    vec(2)
    do_d(2)
    vec(3)
    do_end(1)
    for s in range(4):
        gexp_ref[:, s * D : s * D + D] = FIN[1, s * 96 : s * 96 + 96, :].astype(jnp.float32)
    do_e(2)
    vec(4)
    do_f(2)
    vec(5)
    gvec_ref[...] = VS[5]
    do_end(2)
    for s in range(3):
        gin_ref[:, s * D : s * D + D] = FIN[2, s * 96 : s * 96 + 96, :].astype(jnp.float32)
    gout_ref[...] = FIN[2, 288:384, :].astype(jnp.float32)

    for k in range(5):
        to_y[k].wait_send()
        to_sib[k].wait_send()
        forward[k].wait_send()
        vec_steps[k].wait_send()
    for n in range(3):
        step_a(n).wait_send()
        step_b(n).wait_send()
        for copy in steps_d(n) + steps_e(n):
            copy.wait_send()
        step_f(n).wait_send()


def fused_body(
    images, counts, first_gain, first_shift, project_in, query_bias, value_bias, project_out, output_bias,
    second_gain, second_shift, expand_weight, expand_bias, reduce_weight, reduce_bias, cotangent,
):
    slots, length, width = images.shape
    alive = (jnp.arange(slots) < counts[0]).astype(jnp.float32)
    rows = [first_gain, first_shift, query_bias, value_bias, output_bias, second_gain, second_shift, reduce_bias]
    pack = jnp.concatenate([jnp.stack(rows), expand_bias.reshape(4, 96)], axis=0)
    pack = jnp.pad(pack, ((0, 4), (0, 32)))
    f32, b16 = jnp.float32, jnp.bfloat16
    n = slots * ROWS
    vm = pl.BlockSpec(memory_space=pltpu.VMEM)
    scratch = [
        ((384, 1152), b16), ((384, 384), b16), ((384, 1536), b16), ((1536, 384), b16), ((64, 128), b16),
        ((16, 384), f32), ((8, 384), f32),
        ((n, 384), b16), ((n, 1152), b16), ((slots * HEADS, ROWS, ROWS), f32), ((n, 384), b16), ((n, 384), f32),
        ((n, 384), f32), ((n, 384), f32), ((n, 128), f32), ((n, 128), f32), ((n, 384), b16), ((n, 1536), b16),
        ((n, 1536), f32), ((n, 384), b16), ((n, 1536), b16), ((n, 384), f32), ((n, 384), b16), ((n, 384), b16),
        ((n, 1152), b16),
        ((3, 2, 2, 384, 384), b16), ((3, 2, 384, 384), b16), ((3, 384, 384), b16), ((3, 384, 384), b16),
        ((3, 384, 384), b16), ((3, 192, 384), b16), ((3, 3, 48, 384), b16), ((3, 384, 384), b16), ((3, 384, 384), f32),
        ((6, 16, 384), f32), ((5, 16, 384), f32),
    ]
    outs = pl.pallas_call(
        mega,
        out_shape=[
            jax.ShapeDtypeStruct(images.shape, b16),
            jax.ShapeDtypeStruct(images.shape, b16),
            jax.ShapeDtypeStruct((96, 1152), f32),
            jax.ShapeDtypeStruct((96, 384), f32),
            jax.ShapeDtypeStruct((96, 1536), f32),
            jax.ShapeDtypeStruct((384, 384), f32),
            jax.ShapeDtypeStruct((16, 384), f32),
        ],
        in_specs=[vm, pl.BlockSpec(memory_space=pltpu.SMEM)] + [vm] * 6,
        out_specs=[vm] * 7,
        scratch_shapes=[pltpu.VMEM(shape, kind) for shape, kind in scratch]
        + [
            pltpu.SemaphoreType.DMA((3, 5)),
            pltpu.SemaphoreType.DMA((3, 5)),
            pltpu.SemaphoreType.DMA((4, 10)),
            pltpu.SemaphoreType.DMA((4, 10)),
        ],
        compiler_params=pltpu.CompilerParams(collective_id=0, has_side_effects=True, vmem_limit_bytes=60 * 2**20),
    )(images, alive, cotangent, pack, project_in, project_out, expand_weight, reduce_weight)
    out, ingrad, gin, gout, gexp, gred, gvec = outs
    shard = lax.axis_index("shard")
    part = lax.dynamic_slice(gvec, (0, shard * 96), (8, 96))
    gbe = lax.dynamic_slice(gvec, (8 + shard, 0), (1, 384))[0]
    return (
        out, ingrad, part[0], part[1], gin, part[2], part[3], gout, part[4], part[5], part[6],
        gexp, gbe, gred, part[7],
    )


def solution(mesh):
    fits = mesh.shape["replica"] == 8 and mesh.shape["shard"] == 4
    return jax.shard_map(
        fused_body if fits else body,
        mesh=mesh,
        in_specs=(
            P(("replica", "shard"), None, None),
            P(("replica", "shard")),
            P("shard"),
            P("shard"),
            P("shard", None),
            P("shard"),
            P("shard"),
            P("shard", None),
            P("shard"),
            P("shard"),
            P("shard"),
            P("shard", None),
            P("shard"),
            P("shard", None),
            P("shard"),
            P(("replica", "shard"), None, None),
        ),
        out_specs=(
            P(("replica", "shard"), None, None),
            P(("replica", "shard"), None, None),
            P("shard"),
            P("shard"),
            P("shard", None),
            P("shard"),
            P("shard"),
            P("shard", None),
            P("shard"),
            P("shard"),
            P("shard"),
            P("shard", None),
            P("shard"),
            P("shard", None),
            P("shard"),
        ),
        check_vma=False,
    )
```

```python
import jax
import jax.numpy as jnp
from jax import lax
from jax.experimental import pallas as pl
from jax.experimental.pallas import tpu as pltpu
from jax.sharding import PartitionSpec as P

HEADS = 6
HEAD_DIM = 64


EPS = 1e-06


def layer_norm(hidden_rows, gain_vector, shift_vector):
    center = hidden_rows - jnp.mean(hidden_rows, -1, keepdims=True)
    spread = jnp.mean(center * center, -1, keepdims=True)
    return center * lax.rsqrt(spread + EPS) * gain_vector + shift_vector


def gelu_exact(argument):
    return jax.nn.gelu(argument, approximate=False)


def column_total(gradient):
    return jnp.sum(gradient.astype(jnp.float32), axis=0)


def outer_sum(left, right):
    return lax.dot_general(
        left, right, (((0,), (0,)), ((), ())), preferred_element_type=jnp.float32
    )


def back_product(gradient, weight):
    return lax.dot_general(
        gradient, weight, (((1,), (1,)), ((), ())), preferred_element_type=jnp.float32
    )


def attend_scores(queries, key_rows, score_scale):
    return (
        jnp.einsum("sqhd,skhd->shqk", queries, key_rows, preferred_element_type=jnp.float32)
        * score_scale
    )


def body(
    images,
    counts,
    first_gain,
    first_shift,
    project_in,
    query_bias,
    value_bias,
    project_out,
    output_bias,
    second_gain,
    second_shift,
    expand_weight,
    expand_bias,
    reduce_weight,
    reduce_bias,
    cotangent,
):
    slot_count, length, feature_width = images.shape
    score_scale = HEAD_DIM ** (-0.5)
    head_shape = (slot_count, length, HEADS, HEAD_DIM)
    gathered = (
        lax.all_gather(first_gain, "shard", axis=0, tiled=True),
        lax.all_gather(first_shift, "shard", axis=0, tiled=True),
        lax.all_gather(project_in, "shard", axis=0, tiled=True),
        lax.all_gather(query_bias, "shard", axis=0, tiled=True),
        lax.all_gather(value_bias, "shard", axis=0, tiled=True),
        lax.all_gather(project_out, "shard", axis=0, tiled=True),
        lax.all_gather(output_bias, "shard", axis=0, tiled=True),
        lax.all_gather(second_gain, "shard", axis=0, tiled=True),
        lax.all_gather(second_shift, "shard", axis=0, tiled=True),
        lax.all_gather(expand_weight, "shard", axis=0, tiled=True),
        lax.all_gather(expand_bias, "shard", axis=0, tiled=True),
        lax.all_gather(reduce_weight, "shard", axis=0, tiled=True),
        lax.all_gather(reduce_bias, "shard", axis=0, tiled=True),
    )
    (
        gain_one,
        shift_one,
        inproj_full,
        query_shift,
        value_shift,
        outproj_full,
        out_shift,
        gain_two,
        shift_two,
        expand_full,
        expand_shift,
        reduce_full,
        reduce_shift,
    ) = gathered
    gain_one = gain_one.astype(jnp.float32)
    gain_two = gain_two.astype(jnp.float32)
    alive = (jnp.arange(slot_count) < counts[0]).astype(jnp.float32)
    tokens = images.astype(jnp.float32).reshape(-1, feature_width)
    normed_one = layer_norm(tokens, gain_one, shift_one.astype(jnp.float32)).astype(jnp.bfloat16)
    triple = jnp.dot(normed_one, inproj_full, preferred_element_type=jnp.float32)
    queries = (
        (triple[:, :feature_width] + query_shift.astype(jnp.float32))
        .astype(jnp.bfloat16)
        .reshape(head_shape)
    )
    key_rows = triple[:, feature_width : 2 * feature_width].astype(jnp.bfloat16).reshape(head_shape)
    value_rows = (
        (triple[:, 2 * feature_width :] + value_shift.astype(jnp.float32))
        .astype(jnp.bfloat16)
        .reshape(head_shape)
    )
    scores = attend_scores(queries, key_rows, score_scale)
    row_max = jnp.max(scores, -1, keepdims=True)
    log_total = row_max + jnp.log(jnp.sum(jnp.exp(scores - row_max), -1, keepdims=True))
    attend_weights = jnp.exp(scores - log_total).astype(jnp.bfloat16)
    mixed = jnp.einsum(
        "shqk,skhd->sqhd", attend_weights, value_rows, preferred_element_type=jnp.float32
    )
    mixed = mixed.reshape(-1, feature_width).astype(jnp.bfloat16)
    middle = (
        tokens
        + jnp.dot(mixed, outproj_full, preferred_element_type=jnp.float32)
        + out_shift.astype(jnp.float32)
    )
    normed_two = layer_norm(middle, gain_two, shift_two.astype(jnp.float32)).astype(jnp.bfloat16)
    before_gelu = jnp.dot(
        normed_two, expand_full, preferred_element_type=jnp.float32
    ) + expand_shift.astype(jnp.float32)
    hidden = gelu_exact(before_gelu).astype(jnp.bfloat16)
    result = (
        middle
        + jnp.dot(hidden, reduce_full, preferred_element_type=jnp.float32)
        + reduce_shift.astype(jnp.float32)
    )
    output = (result.reshape(slot_count, length, feature_width) * alive[:, None, None]).astype(
        jnp.bfloat16
    )
    reduce_back, expand_back, gain_two_back, outproj_back, inproj_back, gain_one_back = (
        lax.all_gather(reduce_weight, "shard", axis=0, tiled=True),
        lax.all_gather(expand_weight, "shard", axis=0, tiled=True),
        lax.all_gather(second_gain, "shard", axis=0, tiled=True),
        lax.all_gather(project_out, "shard", axis=0, tiled=True),
        lax.all_gather(project_in, "shard", axis=0, tiled=True),
        lax.all_gather(first_gain, "shard", axis=0, tiled=True),
    )
    gain_two_back = gain_two_back.astype(jnp.float32)
    gain_one_back = gain_one_back.astype(jnp.float32)
    out_grad = (cotangent.astype(jnp.float32) * alive[:, None, None]).reshape(-1, feature_width)
    branch_grad = out_grad.astype(jnp.bfloat16)
    reduce_weight_grad = outer_sum(hidden, branch_grad)
    reduce_bias_grad = column_total(branch_grad)
    hidden_grad = back_product(branch_grad, reduce_back)
    _, gelu_pull = jax.vjp(gelu_exact, before_gelu)
    expand_grad = gelu_pull(hidden_grad)[0].astype(jnp.bfloat16)
    expand_weight_grad = outer_sum(normed_two, expand_grad)
    expand_bias_grad = column_total(expand_grad)
    normed_two_grad = back_product(expand_grad, expand_back)
    _, norm_two_pull = jax.vjp(layer_norm, middle, gain_two_back, jnp.zeros_like(gain_two_back))
    middle_norm_grad, second_gain_grad, second_shift_grad = norm_two_pull(normed_two_grad)
    middle_grad = out_grad + middle_norm_grad
    proj_grad = middle_grad.astype(jnp.bfloat16)
    project_out_grad = outer_sum(mixed, proj_grad)
    output_bias_grad = column_total(proj_grad)
    mixed_grad = back_product(proj_grad, outproj_back).astype(jnp.bfloat16).reshape(head_shape)
    scores_again = attend_scores(queries, key_rows, score_scale)
    probs_exact = jnp.exp(scores_again - log_total)
    probs_round = probs_exact.astype(jnp.bfloat16)
    values_grad = jnp.einsum(
        "shqk,sqhd->skhd", probs_round, mixed_grad, preferred_element_type=jnp.float32
    )
    probs_grad = jnp.einsum(
        "sqhd,skhd->shqk", mixed_grad, value_rows, preferred_element_type=jnp.float32
    )
    scores_grad = probs_exact * (probs_grad - jnp.sum(probs_exact * probs_grad, -1, keepdims=True))
    scores_grad = scores_grad.astype(jnp.bfloat16)
    queries_grad = (
        jnp.einsum("shqk,skhd->sqhd", scores_grad, key_rows, preferred_element_type=jnp.float32)
        * score_scale
    )
    keys_grad = (
        jnp.einsum("shqk,sqhd->skhd", scores_grad, queries, preferred_element_type=jnp.float32)
        * score_scale
    )
    triple_grad = jnp.concatenate(
        (
            queries_grad.reshape(-1, feature_width),
            keys_grad.reshape(-1, feature_width),
            values_grad.reshape(-1, feature_width),
        ),
        axis=1,
    ).astype(jnp.bfloat16)
    project_in_grad = outer_sum(normed_one, triple_grad)
    query_bias_grad = column_total(triple_grad[:, :feature_width])
    value_bias_grad = column_total(triple_grad[:, 2 * feature_width :])
    normed_one_grad = back_product(triple_grad, inproj_back)
    _, norm_one_pull = jax.vjp(layer_norm, tokens, gain_one_back, jnp.zeros_like(gain_one_back))
    tokens_norm_grad, first_gain_grad, first_shift_grad = norm_one_pull(normed_one_grad)
    input_grad = (
        (middle_grad + tokens_norm_grad)
        .reshape(slot_count, length, feature_width)
        .astype(jnp.bfloat16)
    )
    shares = (
        lax.psum_scatter(first_gain_grad, "shard", scatter_dimension=0, tiled=True),
        lax.psum_scatter(first_shift_grad, "shard", scatter_dimension=0, tiled=True),
        lax.psum_scatter(project_in_grad, "shard", scatter_dimension=0, tiled=True),
        lax.psum_scatter(query_bias_grad, "shard", scatter_dimension=0, tiled=True),
        lax.psum_scatter(value_bias_grad, "shard", scatter_dimension=0, tiled=True),
        lax.psum_scatter(project_out_grad, "shard", scatter_dimension=0, tiled=True),
        lax.psum_scatter(output_bias_grad, "shard", scatter_dimension=0, tiled=True),
        lax.psum_scatter(second_gain_grad, "shard", scatter_dimension=0, tiled=True),
        lax.psum_scatter(second_shift_grad, "shard", scatter_dimension=0, tiled=True),
        lax.psum_scatter(expand_weight_grad, "shard", scatter_dimension=0, tiled=True),
        lax.psum_scatter(expand_bias_grad, "shard", scatter_dimension=0, tiled=True),
        lax.psum_scatter(reduce_weight_grad, "shard", scatter_dimension=0, tiled=True),
        lax.psum_scatter(reduce_bias_grad, "shard", scatter_dimension=0, tiled=True),
    )
    totals = tuple(
        lax.psum(
            (
                shares[0],
                shares[1],
                shares[2],
                shares[3],
                shares[4],
                shares[5],
                shares[6],
                shares[7],
                shares[8],
                shares[9],
                shares[10],
                shares[11],
                shares[12],
            ),
            "replica",
        )
    )
    return (
        output,
        input_grad,
        totals[0],
        totals[1],
        totals[2],
        totals[3],
        totals[4],
        totals[5],
        totals[6],
        totals[7],
        totals[8],
        totals[9],
        totals[10],
        totals[11],
        totals[12],
    )


ROWS = 208
MESH = pl.DeviceIdType.MESH


def mm(left, right):
    return jnp.dot(left, right, preferred_element_type=jnp.float32)


def mega(
    images_ref, counts_ref, cot_ref, pack_ref, win_ref, wout_ref, wexp_ref, wred_ref,
    out_ref, ingrad_ref, FIN, gvec_ref,
    WI, WO, WE, WR, VG, VEC, BE,
    A1, QKV, PR, MIX, H1, XH1, XH2, RS1, RS2, A2, HID, GP, DM, DU, DH1, DZ, DMX, DT,
    GB, AR, BS, BR, CS, CR, DR, ACC, V0, V1, V2,
    gss, grs, rss, rrs, vss, vrs,
):
    D = 384
    slots, length, _ = images_ref.shape
    replica, shard = lax.axis_index("replica"), lax.axis_index("shard")
    z, x = replica // 2, replica % 2
    y, c = shard // 2, shard % 2
    sib = (replica, y * 2 + 1 - c)
    ypart = (replica, (1 - y) * 2 + c)
    xpart = (z * 2 + 1 - x, shard)
    zparts = [(((z + d) % 4) * 2 + x, shard) for d in (1, 2, 3)]

    barrier = pltpu.get_barrier_semaphore()
    group = [(replica, (shard + d) % 4) for d in (1, 2, 3)]
    replicas = [((replica + d) % 8, shard) for d in range(1, 8)]
    for who in group + replicas:
        pl.semaphore_signal(barrier, inc=1, device_id=who, device_id_type=MESH)
    pl.semaphore_wait(barrier, 10)

    def remote(src, dst, ss, rs, who):
        return pltpu.make_async_remote_copy(
            src_ref=src, dst_ref=dst, send_sem=ss, recv_sem=rs, device_id=who, device_id_type=MESH
        )

    items = [(pack_ref, VG, 16), (win_ref, WI, 96), (wout_ref, WO, 96), (wexp_ref, WE, 96), (wred_ref, WR, 384)]
    other_y = (1 - y) * 2 + c
    to_y, to_sib, near, to_x, far = [], [], [], [], []
    for k, (src, full, rows) in enumerate(items):
        part = rows // 2 if k else rows
        near_at = x * part if k else 0
        far_at = (1 - x) * part if k else 0
        mine = full.at[pl.ds(pl.multiple_of(shard * rows, 16), rows)]
        sent = full.at[pl.ds(pl.multiple_of(shard * rows + near_at, 16), part)]
        got = full.at[pl.ds(pl.multiple_of(other_y * rows + near_at, 16), part)]
        rest = full.at[pl.ds(pl.multiple_of(other_y * rows + far_at, 16), part)]
        to_y.append(remote(src.at[pl.ds(pl.multiple_of(near_at, 16), part)] if k else src, sent, gss.at[0, k], grs.at[0, k], ypart))
        to_sib.append(remote(src, mine, gss.at[1, k], grs.at[1, k], sib))
        near.append(remote(got, got, gss.at[2, k], grs.at[2, k], sib))
        to_x.append(remote(got, got, gss.at[3, k], grs.at[3, k], xpart))
        far.append(remote(rest, rest, gss.at[4, k], grs.at[4, k], sib))
    for k in range(5):
        to_y[k].start()
    for k in range(5):
        to_sib[k].start()
    for src, full, rows in items:
        full[pl.ds(pl.multiple_of(shard * rows, 16), rows), :] = src[...]

    def relay_y(k):
        to_y[k].wait_recv()
        if k:
            to_x[k].start()
        near[k].start()

    def relay_x(k):
        if k:
            to_x[k].wait_recv()
            far[k].start()

    def settle(k):
        to_sib[k].wait_recv()
        near[k].wait_recv()
        if k:
            far[k].wait_recv()

    for relay in (relay_y, relay_x, settle):
        for k in (0, 1):
            relay(k)
    lane = lax.broadcasted_iota(jnp.int32, (128, D), 1)
    sub = lax.broadcasted_iota(jnp.int32, (128, D), 0)
    place = [jnp.where((lane == sub + 96 * s) & (sub < 96), 1.0, 0.0).astype(jnp.bfloat16) for s in range(4)]
    blocks = [VG[16 * s : 16 * s + 16, :] for s in range(4)]
    VEC[...] = sum(mm(blocks[s], place[s]) for s in range(4))
    for s in range(4):
        BE[s : s + 1, :] = sum(mm(blocks[s], place[k])[8 + k : 9 + k, :] for k in range(4))
    row = lambda j: VEC[j : j + 1, :]
    half = lax.broadcasted_iota(jnp.int32, (ROWS, 128), 1) < 64
    keep = lax.broadcasted_iota(jnp.int32, (ROWS, ROWS), 1) < length
    scale = HEAD_DIM ** (-0.5)
    pairs = HEADS // 2

    def alive(i):
        return jnp.where(i < counts_ref[0], 1.0, 0.0).astype(jnp.float32)

    def at(i):
        return pl.ds(pl.multiple_of(i * ROWS, 16), ROWS)

    def pad(value):
        return jnp.concatenate([value, jnp.zeros((ROWS - length, D), value.dtype)], axis=0)

    def norm(value):
        center = value - jnp.mean(value, -1, keepdims=True)
        inverse = lax.rsqrt(jnp.mean(center * center, -1, keepdims=True) + EPS)
        return center * inverse, inverse

    def norm_back(grad, gain, unit, inverse):
        g = grad * gain
        return inverse * (g - jnp.mean(g, -1, keepdims=True) - unit * jnp.mean(g * unit, -1, keepdims=True))

    def pick(h, value):
        zero = jnp.zeros_like(value)
        return jnp.where(half, value, zero) if h == 0 else jnp.where(half, zero, value)

    def nt(left, right):
        return lax.dot_general(left, right, (((1,), (1,)), ((), ())), preferred_element_type=jnp.float32)

    def tn(left, right):
        return lax.dot_general(left, right, (((0,), (0,)), ((), ())), preferred_element_type=jnp.float32)

    @pl.loop(0, slots)
    def _(i):
        r = at(i)

        @pl.when(i == 1)
        def _():
            relay_y(2)
            relay_y(3)

        @pl.when(i == 2)
        def _():
            relay_x(2)
            relay_x(3)

        tokens = pad(images_ref[i].astype(jnp.float32))
        unit, inverse = norm(tokens)
        H1[r, :] = tokens
        XH1[r, :] = unit
        RS1[r, :] = jnp.broadcast_to(inverse, (ROWS, 128))
        A1[r, :] = (unit * row(0) + row(1)).astype(jnp.bfloat16)
        a1 = A1[r, :]
        QKV[r, 0:D] = (mm(a1, WI[:, 0:D]) + row(2)).astype(jnp.bfloat16)
        QKV[r, D : 2 * D] = mm(a1, WI[:, D : 2 * D]).astype(jnp.bfloat16)
        QKV[r, 2 * D : 3 * D] = (mm(a1, WI[:, 2 * D : 3 * D]) + row(3)).astype(jnp.bfloat16)
        for p in range(pairs):
            q = QKV[r, p * 128 : p * 128 + 128]
            k = QKV[r, D + p * 128 : D + p * 128 + 128]
            v = QKV[r, 2 * D + p * 128 : 2 * D + p * 128 + 128]
            both = []
            for h in range(2):
                scores = jnp.where(keep, nt(pick(h, q), k) * scale, -1e30)
                e = jnp.exp(scores - jnp.max(scores, -1, keepdims=True))
                prob = e * (1.0 / jnp.sum(e, -1, keepdims=True))
                PR[i * HEADS + p * 2 + h] = prob
                both.append(mm(prob.astype(jnp.bfloat16), v))
            MIX[r, p * 128 : p * 128 + 128] = jnp.where(half, both[0], both[1]).astype(jnp.bfloat16)

    settle(2)
    relay_y(4)
    settle(3)

    @pl.loop(0, slots)
    def _(i):
        r = at(i)

        @pl.when(i == 1)
        def _():
            relay_x(4)

        middle = H1[r, :] + mm(MIX[r, :], WO[...]) + row(4)
        H1[r, :] = middle
        unit, inverse = norm(middle)
        XH2[r, :] = unit
        RS2[r, :] = jnp.broadcast_to(inverse, (ROWS, 128))
        A2[r, :] = (unit * row(5) + row(6)).astype(jnp.bfloat16)
        a2 = A2[r, :]
        for s in range(4):
            cols = slice(s * D, s * D + D)
            u = mm(a2, WE[:, cols]) + BE[s : s + 1, :]
            cdf = 0.5 * (1.0 + lax.erf(u * (0.5**0.5)))
            HID[r, cols] = (u * cdf).astype(jnp.bfloat16)
            GP[r, cols] = cdf + u * (jnp.exp(-0.5 * u * u) * 0.3989422804014327)
        DM[r, :] = pad(cot_ref[i].astype(jnp.float32) * alive(i)).astype(jnp.bfloat16)

    settle(4)
    V0[...] = jnp.zeros_like(V0)

    def tally(j, value):
        V0[j : j + 1, :] += jnp.sum(value, axis=0, keepdims=True)

    @pl.loop(0, slots)
    def _(i):
        r = at(i)
        result = H1[r, :] + mm(HID[r, :], WR[...]) + row(7)
        out_ref[i] = (result * alive(i)).astype(jnp.bfloat16)[:length]
        dm = DM[r, :]
        tally(7, dm.astype(jnp.float32))
        for s in range(4):
            cols = slice(s * D, s * D + D)
            du = (nt(dm, WR[cols, :]) * GP[r, cols]).astype(jnp.bfloat16)
            DU[r, cols] = du
            tally(8 + s, du.astype(jnp.float32))

    chunks = [(m, off, size) for m in range(3) for off, size in ((0, 256), (256, 128))]

    def span(n, at_row, size):
        return pl.ds(pl.multiple_of(chunks[n][1] + at_row, 16), size)

    def step_a(n):
        m, off, size = chunks[n]
        rows = pl.ds(off, size)
        return remote(GB.at[m, 1 - c, :, rows], AR.at[m, :, rows], rss.at[n, 0], rrs.at[n, 0], sib)

    def step_b(n):
        m, off, size = chunks[n]
        rows = pl.ds(off, size)
        return remote(BS.at[m, rows], BR.at[m, rows], rss.at[n, 1], rrs.at[n, 1], ypart)

    def step_c(n):
        m, off, size = chunks[n]
        src = CS.at[m, span(n, (1 - x) * (size // 2), size // 2)]
        return remote(src, CR.at[m, pl.ds(off // 2, size // 2)], rss.at[n, 2], rrs.at[n, 2], xpart)

    def steps_d(n):
        m, off, size = chunks[n]
        return [
            remote(CS.at[m, span(n, x * (size // 2) + ((z + d) % 4) * (size // 8), size // 8)],
                   DR.at[m, d - 1, pl.ds(off // 8, size // 8)],
                   rss.at[n, 2 + d], rrs.at[n, 2 + d], zparts[d - 1])
            for d in (1, 2, 3)
        ]

    def steps_e(n):
        m, off, size = chunks[n]
        piece = FIN.at[m, span(n, x * (size // 2) + z * (size // 8), size // 8)]
        return [remote(piece, piece, rss.at[n, 5 + d], rrs.at[n, 5 + d], zparts[d - 1]) for d in (1, 2, 3)]

    def step_f(n):
        m, off, size = chunks[n]
        piece = FIN.at[m, span(n, x * (size // 2), size // 2)]
        return remote(piece, piece, rss.at[n, 9], rrs.at[n, 9], xpart)

    def do_a(n):
        step_a(n).start()

    def do_b(n):
        m, off, size = chunks[n]
        rows = slice(off, off + size)
        step_a(n).wait_recv()
        BS[m, rows, :] = (
            GB[m, c, 1 - y, rows, :].astype(jnp.float32) + AR[m, 1 - y, rows, :].astype(jnp.float32)
        ).astype(jnp.bfloat16)
        step_b(n).start()
        ACC[m, rows, :] = GB[m, c, y, rows, :].astype(jnp.float32) + AR[m, y, rows, :].astype(jnp.float32)

    def do_c(n):
        m, off, size = chunks[n]
        rows = slice(off, off + size)
        step_b(n).wait_recv()
        total = ACC[m, rows, :] + BR[m, rows, :].astype(jnp.float32)
        ACC[m, rows, :] = total
        CS[m, rows, :] = total.astype(jnp.bfloat16)
        step_c(n).start()

    def do_d(n):
        m, off, size = chunks[n]
        step_c(n).wait_recv()
        rows = span(n, x * (size // 2), size // 2)
        total = ACC[m, rows, :] + CR[m, off // 2 : off // 2 + size // 2, :].astype(jnp.float32)
        ACC[m, rows, :] = total
        CS[m, rows, :] = total.astype(jnp.bfloat16)
        for copy in steps_d(n):
            copy.start()

    def do_e(n):
        m, off, size = chunks[n]
        for copy in steps_d(n):
            copy.wait_recv()
        rows = span(n, x * (size // 2) + z * (size // 8), size // 8)
        total = ACC[m, rows, :]
        for d in range(3):
            total = total + DR[m, d, off // 8 : off // 8 + size // 8, :].astype(jnp.float32)
        FIN[m, rows, :] = total.astype(jnp.bfloat16)
        for copy in steps_e(n):
            copy.start()

    def do_f(n):
        for copy in steps_e(n):
            copy.wait_recv()
        step_f(n).start()

    def do_end(n):
        step_f(n).wait_recv()

    stages = [do_a, do_b, do_c, do_d, do_e, do_f, do_end]
    starts = [0, 1, 2, 3, 7, 8]

    def slot(t):
        for n in range(6):
            if 0 <= t - starts[n] < 7:
                stages[t - starts[n]](n)

    def put(n, cols_at, grad):
        rows = grad.shape[0] // 4
        for s in range(4):
            GB[n, s % 2, s // 2, cols_at : cols_at + rows, :] = grad[s * rows : s * rows + rows, :].astype(jnp.bfloat16)

    dm_all = DM[...]
    for s in range(4):
        GB[0, s % 2, s // 2] = tn(HID[:, s * D : s * D + D], dm_all).astype(jnp.bfloat16)
    slot(0)
    slot(1)

    a2_all = A2[...]
    for s in range(4):
        put(1, s * 96, tn(a2_all, DU[:, s * D : s * D + D]))
    slot(2)
    slot(3)

    @pl.loop(0, slots)
    def _(i):
        r = at(i)
        da2 = nt(DU[r, :], WE[...])
        unit = XH2[r, :]
        tally(5, da2 * unit)
        tally(6, da2)
        dh1 = DM[r, :].astype(jnp.float32) + norm_back(da2, row(5), unit, RS2[r, 0:1])
        DH1[r, :] = dh1
        dz = dh1.astype(jnp.bfloat16)
        DZ[r, :] = dz
        tally(4, dz.astype(jnp.float32))
        DMX[r, :] = nt(dz, WO[...]).astype(jnp.bfloat16)

    slot(4)
    put(2, 288, tn(MIX[...], DZ[...]))

    @pl.loop(0, slots)
    def _(i):
        @pl.when(i == 1)
        def _():
            slot(5)

        @pl.when(i == 2)
        def _():
            slot(6)

        r = at(i)
        for p in range(pairs):
            cols = slice(p * 128, p * 128 + 128)
            kcols = slice(D + p * 128, D + p * 128 + 128)
            vcols = slice(2 * D + p * 128, 2 * D + p * 128 + 128)
            q, k, v, dmx = QKV[r, cols], QKV[r, kcols], QKV[r, vcols], DMX[r, cols]
            dq, dk, dv = [], 0.0, 0.0
            for h in range(2):
                prob = PR[i * HEADS + p * 2 + h]
                dmh = pick(h, dmx)
                dv = dv + tn(prob.astype(jnp.bfloat16), dmh)
                dp = nt(dmh, v)
                ds = (prob * (dp - jnp.sum(prob * dp, -1, keepdims=True))).astype(jnp.bfloat16)
                dq.append(mm(ds, k))
                dk = dk + tn(ds, pick(h, q))
            dq = (jnp.where(half, dq[0], dq[1]) * scale).astype(jnp.bfloat16)
            DT[r, cols] = dq
            DT[r, kcols] = (dk * scale).astype(jnp.bfloat16)
            DT[r, vcols] = dv.astype(jnp.bfloat16)
        tally(2, DT[r, 0:D].astype(jnp.float32))
        tally(3, DT[r, 2 * D : 3 * D].astype(jnp.float32))

    a1_all = A1[...]
    for s in range(3):
        put(2, s * 96, tn(a1_all, DT[:, s * D : s * D + D]))
    slot(7)
    slot(8)

    @pl.loop(0, slots)
    def _(i):
        r = at(i)

        @pl.when(i == 1)
        def _():
            slot(9)

        @pl.when(i == 2)
        def _():
            slot(10)

        da1 = nt(DT[r, :], WI[...])
        unit = XH1[r, :]
        tally(0, da1 * unit)
        tally(1, da1)
        grad = DH1[r, :] + norm_back(da1, row(0), unit, RS1[r, 0:1])
        ingrad_ref[i] = grad.astype(jnp.bfloat16)[:length]

    group_sends = [
        remote(V0, V1.at[shard], vss.at[d], vrs.at[d], who) for d, who in enumerate(group)
    ]
    for copy in group_sends:
        copy.start()
    V1[shard] = V0[...]
    slot(11)
    for copy in group_sends:
        copy.wait_recv()
    V2[replica] = V1[0] + V1[1] + V1[2] + V1[3]
    replica_sends = [
        remote(V2.at[replica], V2.at[replica], vss.at[3 + d], vrs.at[3 + d], who) for d, who in enumerate(replicas)
    ]
    for copy in replica_sends:
        copy.start()
    slot(12)
    slot(13)
    for copy in replica_sends:
        copy.wait_recv()
    gvec_ref[...] = sum([V2[k] for k in range(1, 8)], V2[0])
    slot(14)

    for k in range(5):
        to_y[k].wait_send()
        to_sib[k].wait_send()
        near[k].wait_send()
        if k:
            to_x[k].wait_send()
            far[k].wait_send()
    for copy in group_sends + replica_sends:
        copy.wait_send()
    for n in range(6):
        step_a(n).wait_send()
        step_b(n).wait_send()
        step_c(n).wait_send()
        for copy in steps_d(n) + steps_e(n):
            copy.wait_send()
        step_f(n).wait_send()


def finish(
    out_in, ingrad_in, sums, vectors, out_ref, ingrad_ref, gin_ref, gout_ref, gexp_ref, gred_ref, gbe_ref, *rest
):
    D = 384
    vector_refs, sem = rest[:8], rest[8]
    copies = [
        pltpu.make_async_copy(out_in, out_ref, sem.at[0]),
        pltpu.make_async_copy(ingrad_in, ingrad_ref, sem.at[1]),
    ]
    for copy in copies:
        copy.start()
    shard = lax.axis_index("shard")
    mine, expand = jnp.zeros((8, 96), jnp.float32), jnp.zeros((1, D), jnp.float32)
    for s in range(4):
        chosen = jnp.where(shard == s, 1.0, 0.0).astype(jnp.float32)
        mine = mine + chosen * vectors[0:8, s * 96 : s * 96 + 96]
        expand = expand + chosen * vectors[8 + s : 9 + s, :]
    for j in range(8):
        vector_refs[j][...] = mine[j : j + 1, :]
    gbe_ref[...] = expand
    gred_ref[...] = sums[0].astype(jnp.float32)
    for s in range(4):
        gexp_ref[:, s * D : s * D + D] = sums[1, s * 96 : s * 96 + 96, :].astype(jnp.float32)
    for s in range(3):
        gin_ref[:, s * D : s * D + D] = sums[2, s * 96 : s * 96 + 96, :].astype(jnp.float32)
    gout_ref[...] = sums[2, 288:384, :].astype(jnp.float32)
    for copy in copies:
        copy.wait()


def fused_body(
    images, counts, first_gain, first_shift, project_in, query_bias, value_bias, project_out, output_bias,
    second_gain, second_shift, expand_weight, expand_bias, reduce_weight, reduce_bias, cotangent,
):
    slots, length, width = images.shape
    rows = [first_gain, first_shift, query_bias, value_bias, output_bias, second_gain, second_shift, reduce_bias]
    pack = jnp.concatenate([jnp.stack(rows), expand_bias.reshape(4, 96)], axis=0)
    pack = jnp.pad(pack, ((0, 4), (0, 32)))
    f32, b16 = jnp.float32, jnp.bfloat16
    n = slots * ROWS
    vm = pl.BlockSpec(memory_space=pltpu.VMEM)
    scratch = [
        ((384, 1152), b16), ((384, 384), b16), ((384, 1536), b16), ((1536, 384), b16), ((64, 128), b16),
        ((16, 384), f32), ((8, 384), f32),
        ((n, 384), b16), ((n, 1152), b16), ((slots * HEADS, ROWS, ROWS), f32), ((n, 384), b16), ((n, 384), f32),
        ((n, 384), f32), ((n, 384), f32), ((n, 128), f32), ((n, 128), f32), ((n, 384), b16), ((n, 1536), b16),
        ((n, 1536), f32), ((n, 384), b16), ((n, 1536), b16), ((n, 384), f32), ((n, 384), b16), ((n, 384), b16),
        ((n, 1152), b16),
        ((3, 2, 2, 384, 384), b16), ((3, 2, 384, 384), b16), ((3, 384, 384), b16), ((3, 384, 384), b16),
        ((3, 384, 384), b16), ((3, 192, 384), b16), ((3, 3, 48, 384), b16), ((3, 384, 384), f32),
        ((16, 384), f32), ((4, 16, 384), f32), ((8, 16, 384), f32),
    ]
    outs = pl.pallas_call(
        mega,
        out_shape=[
            jax.ShapeDtypeStruct(images.shape, b16),
            jax.ShapeDtypeStruct(images.shape, b16),
            jax.ShapeDtypeStruct((3, 384, 384), b16),
            jax.ShapeDtypeStruct((16, 384), f32),
        ],
        in_specs=[vm, pl.BlockSpec(memory_space=pltpu.SMEM)] + [vm] * 6,
        out_specs=[vm] * 4,
        scratch_shapes=[pltpu.VMEM(shape, kind) for shape, kind in scratch]
        + [
            pltpu.SemaphoreType.DMA((5, 5)),
            pltpu.SemaphoreType.DMA((5, 5)),
            pltpu.SemaphoreType.DMA((6, 10)),
            pltpu.SemaphoreType.DMA((6, 10)),
            pltpu.SemaphoreType.DMA((10,)),
            pltpu.SemaphoreType.DMA((10,)),
        ],
        compiler_params=pltpu.CompilerParams(collective_id=0, has_side_effects=True, vmem_limit_bytes=60 * 2**20),
    )(images, counts, cotangent, pack, project_in, project_out, expand_weight, reduce_weight)
    anywhere = pl.BlockSpec(memory_space=pl.ANY)
    vector = jax.ShapeDtypeStruct((1, 96), f32)
    done = pl.pallas_call(
        finish,
        out_shape=[
            jax.ShapeDtypeStruct(images.shape, b16),
            jax.ShapeDtypeStruct(images.shape, b16),
            jax.ShapeDtypeStruct((96, 1152), f32),
            jax.ShapeDtypeStruct((96, 384), f32),
            jax.ShapeDtypeStruct((96, 1536), f32),
            jax.ShapeDtypeStruct((384, 384), f32),
            jax.ShapeDtypeStruct((1, 384), f32),
        ]
        + [vector] * 8,
        in_specs=[anywhere, anywhere, vm, vm],
        out_specs=[anywhere, anywhere] + [vm] * 13,
        scratch_shapes=[pltpu.SemaphoreType.DMA((2,))],
        compiler_params=pltpu.CompilerParams(vmem_limit_bytes=32 * 2**20),
    )(*outs)
    out, ingrad, gin, gout, gexp, gred, gbe = done[:7]
    v = [item.reshape(96) for item in done[7:]]
    return (
        out, ingrad, v[0], v[1], gin, v[2], v[3], gout, v[4], v[5], v[6], gexp, gbe.reshape(384), gred, v[7],
    )


def solution(mesh):
    fits = mesh.shape["replica"] == 8 and mesh.shape["shard"] == 4
    return jax.shard_map(
        fused_body if fits else body,
        mesh=mesh,
        in_specs=(
            P(("replica", "shard"), None, None),
            P(("replica", "shard")),
            P("shard"),
            P("shard"),
            P("shard", None),
            P("shard"),
            P("shard"),
            P("shard", None),
            P("shard"),
            P("shard"),
            P("shard"),
            P("shard", None),
            P("shard"),
            P("shard", None),
            P("shard"),
            P(("replica", "shard"), None, None),
        ),
        out_specs=(
            P(("replica", "shard"), None, None),
            P(("replica", "shard"), None, None),
            P("shard"),
            P("shard"),
            P("shard", None),
            P("shard"),
            P("shard"),
            P("shard", None),
            P("shard"),
            P("shard"),
            P("shard"),
            P("shard", None),
            P("shard"),
            P("shard", None),
            P("shard"),
        ),
        check_vma=False,
    )
```

```python
import jax
import jax.numpy as jnp
from jax import lax
from jax.experimental import pallas as pl
from jax.experimental.pallas import tpu as pltpu
from jax.sharding import PartitionSpec as P

HEADS = 6
HEAD_DIM = 64


EPS = 1e-06


def layer_norm(hidden_rows, gain_vector, shift_vector):
    center = hidden_rows - jnp.mean(hidden_rows, -1, keepdims=True)
    spread = jnp.mean(center * center, -1, keepdims=True)
    return center * lax.rsqrt(spread + EPS) * gain_vector + shift_vector


def gelu_exact(argument):
    return jax.nn.gelu(argument, approximate=False)


def column_total(gradient):
    return jnp.sum(gradient.astype(jnp.float32), axis=0)


def outer_sum(left, right):
    return lax.dot_general(
        left, right, (((0,), (0,)), ((), ())), preferred_element_type=jnp.float32
    )


def back_product(gradient, weight):
    return lax.dot_general(
        gradient, weight, (((1,), (1,)), ((), ())), preferred_element_type=jnp.float32
    )


def attend_scores(queries, key_rows, score_scale):
    return (
        jnp.einsum("sqhd,skhd->shqk", queries, key_rows, preferred_element_type=jnp.float32)
        * score_scale
    )


def body(
    images,
    counts,
    first_gain,
    first_shift,
    project_in,
    query_bias,
    value_bias,
    project_out,
    output_bias,
    second_gain,
    second_shift,
    expand_weight,
    expand_bias,
    reduce_weight,
    reduce_bias,
    cotangent,
):
    slot_count, length, feature_width = images.shape
    score_scale = HEAD_DIM ** (-0.5)
    head_shape = (slot_count, length, HEADS, HEAD_DIM)
    gathered = (
        lax.all_gather(first_gain, "shard", axis=0, tiled=True),
        lax.all_gather(first_shift, "shard", axis=0, tiled=True),
        lax.all_gather(project_in, "shard", axis=0, tiled=True),
        lax.all_gather(query_bias, "shard", axis=0, tiled=True),
        lax.all_gather(value_bias, "shard", axis=0, tiled=True),
        lax.all_gather(project_out, "shard", axis=0, tiled=True),
        lax.all_gather(output_bias, "shard", axis=0, tiled=True),
        lax.all_gather(second_gain, "shard", axis=0, tiled=True),
        lax.all_gather(second_shift, "shard", axis=0, tiled=True),
        lax.all_gather(expand_weight, "shard", axis=0, tiled=True),
        lax.all_gather(expand_bias, "shard", axis=0, tiled=True),
        lax.all_gather(reduce_weight, "shard", axis=0, tiled=True),
        lax.all_gather(reduce_bias, "shard", axis=0, tiled=True),
    )
    (
        gain_one,
        shift_one,
        inproj_full,
        query_shift,
        value_shift,
        outproj_full,
        out_shift,
        gain_two,
        shift_two,
        expand_full,
        expand_shift,
        reduce_full,
        reduce_shift,
    ) = gathered
    gain_one = gain_one.astype(jnp.float32)
    gain_two = gain_two.astype(jnp.float32)
    alive = (jnp.arange(slot_count) < counts[0]).astype(jnp.float32)
    tokens = images.astype(jnp.float32).reshape(-1, feature_width)
    normed_one = layer_norm(tokens, gain_one, shift_one.astype(jnp.float32)).astype(jnp.bfloat16)
    triple = jnp.dot(normed_one, inproj_full, preferred_element_type=jnp.float32)
    queries = (
        (triple[:, :feature_width] + query_shift.astype(jnp.float32))
        .astype(jnp.bfloat16)
        .reshape(head_shape)
    )
    key_rows = triple[:, feature_width : 2 * feature_width].astype(jnp.bfloat16).reshape(head_shape)
    value_rows = (
        (triple[:, 2 * feature_width :] + value_shift.astype(jnp.float32))
        .astype(jnp.bfloat16)
        .reshape(head_shape)
    )
    scores = attend_scores(queries, key_rows, score_scale)
    row_max = jnp.max(scores, -1, keepdims=True)
    log_total = row_max + jnp.log(jnp.sum(jnp.exp(scores - row_max), -1, keepdims=True))
    attend_weights = jnp.exp(scores - log_total).astype(jnp.bfloat16)
    mixed = jnp.einsum(
        "shqk,skhd->sqhd", attend_weights, value_rows, preferred_element_type=jnp.float32
    )
    mixed = mixed.reshape(-1, feature_width).astype(jnp.bfloat16)
    middle = (
        tokens
        + jnp.dot(mixed, outproj_full, preferred_element_type=jnp.float32)
        + out_shift.astype(jnp.float32)
    )
    normed_two = layer_norm(middle, gain_two, shift_two.astype(jnp.float32)).astype(jnp.bfloat16)
    before_gelu = jnp.dot(
        normed_two, expand_full, preferred_element_type=jnp.float32
    ) + expand_shift.astype(jnp.float32)
    hidden = gelu_exact(before_gelu).astype(jnp.bfloat16)
    result = (
        middle
        + jnp.dot(hidden, reduce_full, preferred_element_type=jnp.float32)
        + reduce_shift.astype(jnp.float32)
    )
    output = (result.reshape(slot_count, length, feature_width) * alive[:, None, None]).astype(
        jnp.bfloat16
    )
    reduce_back, expand_back, gain_two_back, outproj_back, inproj_back, gain_one_back = (
        lax.all_gather(reduce_weight, "shard", axis=0, tiled=True),
        lax.all_gather(expand_weight, "shard", axis=0, tiled=True),
        lax.all_gather(second_gain, "shard", axis=0, tiled=True),
        lax.all_gather(project_out, "shard", axis=0, tiled=True),
        lax.all_gather(project_in, "shard", axis=0, tiled=True),
        lax.all_gather(first_gain, "shard", axis=0, tiled=True),
    )
    gain_two_back = gain_two_back.astype(jnp.float32)
    gain_one_back = gain_one_back.astype(jnp.float32)
    out_grad = (cotangent.astype(jnp.float32) * alive[:, None, None]).reshape(-1, feature_width)
    branch_grad = out_grad.astype(jnp.bfloat16)
    reduce_weight_grad = outer_sum(hidden, branch_grad)
    reduce_bias_grad = column_total(branch_grad)
    hidden_grad = back_product(branch_grad, reduce_back)
    _, gelu_pull = jax.vjp(gelu_exact, before_gelu)
    expand_grad = gelu_pull(hidden_grad)[0].astype(jnp.bfloat16)
    expand_weight_grad = outer_sum(normed_two, expand_grad)
    expand_bias_grad = column_total(expand_grad)
    normed_two_grad = back_product(expand_grad, expand_back)
    _, norm_two_pull = jax.vjp(layer_norm, middle, gain_two_back, jnp.zeros_like(gain_two_back))
    middle_norm_grad, second_gain_grad, second_shift_grad = norm_two_pull(normed_two_grad)
    middle_grad = out_grad + middle_norm_grad
    proj_grad = middle_grad.astype(jnp.bfloat16)
    project_out_grad = outer_sum(mixed, proj_grad)
    output_bias_grad = column_total(proj_grad)
    mixed_grad = back_product(proj_grad, outproj_back).astype(jnp.bfloat16).reshape(head_shape)
    scores_again = attend_scores(queries, key_rows, score_scale)
    probs_exact = jnp.exp(scores_again - log_total)
    probs_round = probs_exact.astype(jnp.bfloat16)
    values_grad = jnp.einsum(
        "shqk,sqhd->skhd", probs_round, mixed_grad, preferred_element_type=jnp.float32
    )
    probs_grad = jnp.einsum(
        "sqhd,skhd->shqk", mixed_grad, value_rows, preferred_element_type=jnp.float32
    )
    scores_grad = probs_exact * (probs_grad - jnp.sum(probs_exact * probs_grad, -1, keepdims=True))
    scores_grad = scores_grad.astype(jnp.bfloat16)
    queries_grad = (
        jnp.einsum("shqk,skhd->sqhd", scores_grad, key_rows, preferred_element_type=jnp.float32)
        * score_scale
    )
    keys_grad = (
        jnp.einsum("shqk,sqhd->skhd", scores_grad, queries, preferred_element_type=jnp.float32)
        * score_scale
    )
    triple_grad = jnp.concatenate(
        (
            queries_grad.reshape(-1, feature_width),
            keys_grad.reshape(-1, feature_width),
            values_grad.reshape(-1, feature_width),
        ),
        axis=1,
    ).astype(jnp.bfloat16)
    project_in_grad = outer_sum(normed_one, triple_grad)
    query_bias_grad = column_total(triple_grad[:, :feature_width])
    value_bias_grad = column_total(triple_grad[:, 2 * feature_width :])
    normed_one_grad = back_product(triple_grad, inproj_back)
    _, norm_one_pull = jax.vjp(layer_norm, tokens, gain_one_back, jnp.zeros_like(gain_one_back))
    tokens_norm_grad, first_gain_grad, first_shift_grad = norm_one_pull(normed_one_grad)
    input_grad = (
        (middle_grad + tokens_norm_grad)
        .reshape(slot_count, length, feature_width)
        .astype(jnp.bfloat16)
    )
    shares = (
        lax.psum_scatter(first_gain_grad, "shard", scatter_dimension=0, tiled=True),
        lax.psum_scatter(first_shift_grad, "shard", scatter_dimension=0, tiled=True),
        lax.psum_scatter(project_in_grad, "shard", scatter_dimension=0, tiled=True),
        lax.psum_scatter(query_bias_grad, "shard", scatter_dimension=0, tiled=True),
        lax.psum_scatter(value_bias_grad, "shard", scatter_dimension=0, tiled=True),
        lax.psum_scatter(project_out_grad, "shard", scatter_dimension=0, tiled=True),
        lax.psum_scatter(output_bias_grad, "shard", scatter_dimension=0, tiled=True),
        lax.psum_scatter(second_gain_grad, "shard", scatter_dimension=0, tiled=True),
        lax.psum_scatter(second_shift_grad, "shard", scatter_dimension=0, tiled=True),
        lax.psum_scatter(expand_weight_grad, "shard", scatter_dimension=0, tiled=True),
        lax.psum_scatter(expand_bias_grad, "shard", scatter_dimension=0, tiled=True),
        lax.psum_scatter(reduce_weight_grad, "shard", scatter_dimension=0, tiled=True),
        lax.psum_scatter(reduce_bias_grad, "shard", scatter_dimension=0, tiled=True),
    )
    totals = tuple(
        lax.psum(
            (
                shares[0],
                shares[1],
                shares[2],
                shares[3],
                shares[4],
                shares[5],
                shares[6],
                shares[7],
                shares[8],
                shares[9],
                shares[10],
                shares[11],
                shares[12],
            ),
            "replica",
        )
    )
    return (
        output,
        input_grad,
        totals[0],
        totals[1],
        totals[2],
        totals[3],
        totals[4],
        totals[5],
        totals[6],
        totals[7],
        totals[8],
        totals[9],
        totals[10],
        totals[11],
        totals[12],
    )


ROWS = 208
MESH = pl.DeviceIdType.MESH


def mm(left, right):
    return jnp.dot(left, right, preferred_element_type=jnp.float32)


def mega(
    images_ref, counts_ref, cot_ref, pack_ref, win_ref, wout_ref, wexp_ref, wred_ref,
    out_ref, ingrad_ref, FIN, gvec_ref,
    WI, WO, WE, WR, VG, VEC, BE,
    A1, QKV, PR, MIX, H1, XH1, XH2, RS1, RS2, A2, HID, GP, DM, DU, DH1, DZ, DMX, DT,
    GB, AR, BS, BR, CS, CR, DR, ACC, VS, VR,
    gss, grs, rss, rrs,
):
    D = 384
    slots, length, _ = images_ref.shape
    replica, shard = lax.axis_index("replica"), lax.axis_index("shard")
    z, x = replica // 2, replica % 2
    y, c = shard // 2, shard % 2
    sib = (replica, y * 2 + 1 - c)
    ypart = (replica, (1 - y) * 2 + c)
    xpart = (z * 2 + 1 - x, shard)
    zparts = [(((z + d) % 4) * 2 + x, shard) for d in (1, 2, 3)]

    barrier = pltpu.get_barrier_semaphore()
    for who in [sib, ypart, xpart] + zparts:
        pl.semaphore_signal(barrier, inc=1, device_id=who, device_id_type=MESH)
    pl.semaphore_wait(barrier, 6)

    def remote(src, dst, ss, rs, who):
        return pltpu.make_async_remote_copy(
            src_ref=src, dst_ref=dst, send_sem=ss, recv_sem=rs, device_id=who, device_id_type=MESH
        )

    items = [(pack_ref, VG, 16), (win_ref, WI, 96), (wout_ref, WO, 96), (wexp_ref, WE, 96), (wred_ref, WR, 384)]
    other_y = (1 - y) * 2 + c
    to_y, to_sib, forward = [], [], []
    for k, (src, full, rows) in enumerate(items):
        mine = full.at[pl.ds(pl.multiple_of(shard * rows, 16), rows)]
        theirs = full.at[pl.ds(pl.multiple_of(other_y * rows, 16), rows)]
        to_y.append(remote(src, mine, gss.at[0, k], grs.at[0, k], ypart))
        to_sib.append(remote(src, mine, gss.at[1, k], grs.at[1, k], sib))
        forward.append(remote(theirs, theirs, gss.at[2, k], grs.at[2, k], sib))
    for k in range(5):
        to_y[k].start()
        to_sib[k].start()
    for src, full, rows in items:
        full[pl.ds(pl.multiple_of(shard * rows, 16), rows), :] = src[...]

    def relay(k):
        to_y[k].wait_recv()
        forward[k].start()

    def arrived(ks):
        for k in ks:
            to_sib[k].wait_recv()
            forward[k].wait_recv()

    relay(0)
    relay(1)
    arrived([0, 1])
    lane = lax.broadcasted_iota(jnp.int32, (128, D), 1)
    sub = lax.broadcasted_iota(jnp.int32, (128, D), 0)
    place = [jnp.where((lane == sub + 96 * s) & (sub < 96), 1.0, 0.0).astype(jnp.bfloat16) for s in range(4)]
    blocks = [VG[16 * s : 16 * s + 16, :] for s in range(4)]
    VEC[...] = sum(mm(blocks[s], place[s]) for s in range(4))
    for s in range(4):
        BE[s : s + 1, :] = sum(mm(blocks[s], place[k])[8 + k : 9 + k, :] for k in range(4))
    row = lambda j: VEC[j : j + 1, :]
    half = lax.broadcasted_iota(jnp.int32, (ROWS, 128), 1) < 64
    keep = lax.broadcasted_iota(jnp.int32, (ROWS, ROWS), 1) < length
    scale = HEAD_DIM ** (-0.5)
    pairs = HEADS // 2

    def alive(i):
        return jnp.where(i < counts_ref[0], 1.0, 0.0).astype(jnp.float32)

    def at(i):
        return pl.ds(pl.multiple_of(i * ROWS, 16), ROWS)

    def pad(value):
        return jnp.concatenate([value, jnp.zeros((ROWS - length, D), value.dtype)], axis=0)

    def norm(value):
        center = value - jnp.mean(value, -1, keepdims=True)
        inverse = lax.rsqrt(jnp.mean(center * center, -1, keepdims=True) + EPS)
        return center * inverse, inverse

    def norm_back(grad, gain, unit, inverse):
        g = grad * gain
        return inverse * (g - jnp.mean(g, -1, keepdims=True) - unit * jnp.mean(g * unit, -1, keepdims=True))

    def pick(h, value):
        zero = jnp.zeros_like(value)
        return jnp.where(half, value, zero) if h == 0 else jnp.where(half, zero, value)

    def nt(left, right):
        return lax.dot_general(left, right, (((1,), (1,)), ((), ())), preferred_element_type=jnp.float32)

    def tn(left, right):
        return lax.dot_general(left, right, (((0,), (0,)), ((), ())), preferred_element_type=jnp.float32)

    @pl.loop(0, slots)
    def _(i):
        r = at(i)

        @pl.when(i == 1)
        def _():
            relay(2)

        @pl.when(i == 2)
        def _():
            relay(3)

        tokens = pad(images_ref[i].astype(jnp.float32))
        unit, inverse = norm(tokens)
        H1[r, :] = tokens
        XH1[r, :] = unit
        RS1[r, :] = jnp.broadcast_to(inverse, (ROWS, 128))
        A1[r, :] = (unit * row(0) + row(1)).astype(jnp.bfloat16)
        a1 = A1[r, :]
        QKV[r, 0:D] = (mm(a1, WI[:, 0:D]) + row(2)).astype(jnp.bfloat16)
        QKV[r, D : 2 * D] = mm(a1, WI[:, D : 2 * D]).astype(jnp.bfloat16)
        QKV[r, 2 * D : 3 * D] = (mm(a1, WI[:, 2 * D : 3 * D]) + row(3)).astype(jnp.bfloat16)
        for p in range(pairs):
            q = QKV[r, p * 128 : p * 128 + 128]
            k = QKV[r, D + p * 128 : D + p * 128 + 128]
            v = QKV[r, 2 * D + p * 128 : 2 * D + p * 128 + 128]
            both = []
            for h in range(2):
                scores = jnp.where(keep, nt(pick(h, q), k) * scale, -1e30)
                e = jnp.exp(scores - jnp.max(scores, -1, keepdims=True))
                prob = e * (1.0 / jnp.sum(e, -1, keepdims=True))
                PR[i * HEADS + p * 2 + h] = prob
                both.append(mm(prob.astype(jnp.bfloat16), v))
            MIX[r, p * 128 : p * 128 + 128] = jnp.where(half, both[0], both[1]).astype(jnp.bfloat16)

    arrived([2, 3])

    @pl.loop(0, slots)
    def _(i):
        r = at(i)

        @pl.when(i == 1)
        def _():
            relay(4)

        middle = H1[r, :] + mm(MIX[r, :], WO[...]) + row(4)
        H1[r, :] = middle
        unit, inverse = norm(middle)
        XH2[r, :] = unit
        RS2[r, :] = jnp.broadcast_to(inverse, (ROWS, 128))
        A2[r, :] = (unit * row(5) + row(6)).astype(jnp.bfloat16)
        a2 = A2[r, :]
        for s in range(4):
            cols = slice(s * D, s * D + D)
            u = mm(a2, WE[:, cols]) + BE[s : s + 1, :]
            cdf = 0.5 * (1.0 + lax.erf(u * (0.5**0.5)))
            HID[r, cols] = (u * cdf).astype(jnp.bfloat16)
            GP[r, cols] = cdf + u * (jnp.exp(-0.5 * u * u) * 0.3989422804014327)
        DM[r, :] = pad(cot_ref[i].astype(jnp.float32) * alive(i)).astype(jnp.bfloat16)

    arrived([4])
    VS[...] = jnp.zeros_like(VS)

    def tally(j, value):
        VS[0, j : j + 1, :] += jnp.sum(value, axis=0, keepdims=True)

    @pl.loop(0, slots)
    def _(i):
        r = at(i)
        result = H1[r, :] + mm(HID[r, :], WR[...]) + row(7)
        out_ref[i] = (result * alive(i)).astype(jnp.bfloat16)[:length]
        dm = DM[r, :]
        tally(7, dm.astype(jnp.float32))
        for s in range(4):
            cols = slice(s * D, s * D + D)
            du = (nt(dm, WR[cols, :]) * GP[r, cols]).astype(jnp.bfloat16)
            DU[r, cols] = du
            tally(8 + s, du.astype(jnp.float32))

    def step_a(n):
        return remote(GB.at[n, 1 - c], AR.at[n], rss.at[n, 0], rrs.at[n, 0], sib)

    def step_b(n):
        return remote(BS.at[n], BR.at[n], rss.at[n, 1], rrs.at[n, 1], ypart)

    def step_c(n):
        return remote(CS.at[n, pl.ds(pl.multiple_of((1 - x) * 192, 16), 192)], CR.at[n], rss.at[n, 2], rrs.at[n, 2], xpart)

    def steps_d(n):
        return [
            remote(CS.at[n, pl.ds(pl.multiple_of(x * 192 + ((z + d) % 4) * 48, 16), 48)], DR.at[n, d - 1],
                   rss.at[n, 2 + d], rrs.at[n, 2 + d], zparts[d - 1])
            for d in (1, 2, 3)
        ]

    def steps_e(n):
        piece = FIN.at[n, pl.ds(pl.multiple_of(x * 192 + z * 48, 16), 48)]
        return [remote(piece, piece, rss.at[n, 5 + d], rrs.at[n, 5 + d], zparts[d - 1]) for d in (1, 2, 3)]

    def step_f(n):
        piece = FIN.at[n, pl.ds(pl.multiple_of(x * 192, 16), 192)]
        return remote(piece, piece, rss.at[n, 9], rrs.at[n, 9], xpart)

    def do_a(n):
        step_a(n).start()

    def do_b(n):
        step_a(n).wait_recv()
        BS[n] = (GB[n, c, 1 - y].astype(jnp.float32) + AR[n, 1 - y].astype(jnp.float32)).astype(jnp.bfloat16)
        step_b(n).start()
        ACC[n] = GB[n, c, y].astype(jnp.float32) + AR[n, y].astype(jnp.float32)

    def do_c(n):
        step_b(n).wait_recv()
        total = ACC[n] + BR[n].astype(jnp.float32)
        ACC[n] = total
        CS[n] = total.astype(jnp.bfloat16)
        step_c(n).start()

    def do_d(n):
        step_c(n).wait_recv()
        step_c(n).wait_send()
        rows = pl.ds(pl.multiple_of(x * 192, 16), 192)
        total = ACC[n, rows, :] + CR[n].astype(jnp.float32)
        ACC[n, rows, :] = total
        CS[n, rows, :] = total.astype(jnp.bfloat16)
        for copy in steps_d(n):
            copy.start()

    def do_e(n):
        for copy in steps_d(n):
            copy.wait_recv()
        rows = pl.ds(pl.multiple_of(x * 192 + z * 48, 16), 48)
        total = ACC[n, rows, :] + DR[n, 0].astype(jnp.float32) + DR[n, 1].astype(jnp.float32) + DR[n, 2].astype(jnp.float32)
        FIN[n, rows, :] = total.astype(jnp.bfloat16)
        for copy in steps_e(n):
            copy.start()

    def do_f(n):
        for copy in steps_e(n):
            copy.wait_recv()
        step_f(n).start()

    def do_end(n):
        step_f(n).wait_recv()

    def put(n, cols_at, grad):
        rows = grad.shape[0] // 4
        for s in range(4):
            GB[n, s % 2, s // 2, cols_at : cols_at + rows, :] = grad[s * rows : s * rows + rows, :].astype(jnp.bfloat16)

    dm_all = DM[...]
    for s in range(4):
        GB[0, s % 2, s // 2] = tn(HID[:, s * D : s * D + D], dm_all).astype(jnp.bfloat16)
    do_a(0)

    a2_all = A2[...]
    for s in range(4):
        put(1, s * 96, tn(a2_all, DU[:, s * D : s * D + D]))
    do_b(0)
    do_a(1)

    @pl.loop(0, slots)
    def _(i):
        r = at(i)
        da2 = nt(DU[r, :], WE[...])
        unit = XH2[r, :]
        tally(5, da2 * unit)
        tally(6, da2)
        dh1 = DM[r, :].astype(jnp.float32) + norm_back(da2, row(5), unit, RS2[r, 0:1])
        DH1[r, :] = dh1
        dz = dh1.astype(jnp.bfloat16)
        DZ[r, :] = dz
        tally(4, dz.astype(jnp.float32))
        DMX[r, :] = nt(dz, WO[...]).astype(jnp.bfloat16)

    do_b(1)
    put(2, 288, tn(MIX[...], DZ[...]))

    def attend_back(i):
        r = at(i)
        for p in range(pairs):
            cols = slice(p * 128, p * 128 + 128)
            kcols = slice(D + p * 128, D + p * 128 + 128)
            vcols = slice(2 * D + p * 128, 2 * D + p * 128 + 128)
            q, k, v, dmx = QKV[r, cols], QKV[r, kcols], QKV[r, vcols], DMX[r, cols]
            dq, dk, dv = [], 0.0, 0.0
            for h in range(2):
                prob = PR[i * HEADS + p * 2 + h]
                dmh = pick(h, dmx)
                dv = dv + tn(prob.astype(jnp.bfloat16), dmh)
                dp = nt(dmh, v)
                ds = (prob * (dp - jnp.sum(prob * dp, -1, keepdims=True))).astype(jnp.bfloat16)
                dq.append(mm(ds, k))
                dk = dk + tn(ds, pick(h, q))
            dq = (jnp.where(half, dq[0], dq[1]) * scale).astype(jnp.bfloat16)
            DT[r, cols] = dq
            DT[r, kcols] = (dk * scale).astype(jnp.bfloat16)
            DT[r, vcols] = dv.astype(jnp.bfloat16)
        tally(2, DT[r, 0:D].astype(jnp.float32))
        tally(3, DT[r, 2 * D : 3 * D].astype(jnp.float32))

    @pl.loop(0, 1)
    def _(i):
        attend_back(i)

    do_c(0)

    @pl.loop(1, 2)
    def _(i):
        attend_back(i)

    do_d(0)
    do_c(1)

    @pl.loop(2, slots)
    def _(i):
        attend_back(i)

    do_e(0)
    do_d(1)
    a1_all = A1[...]
    for s in range(3):
        put(2, s * 96, tn(a1_all, DT[:, s * D : s * D + D]))
    do_a(2)
    do_f(0)
    do_e(1)

    @pl.loop(0, slots)
    def _(i):
        r = at(i)
        da1 = nt(DT[r, :], WI[...])
        unit = XH1[r, :]
        tally(0, da1 * unit)
        tally(1, da1)
        grad = DH1[r, :] + norm_back(da1, row(0), unit, RS1[r, 0:1])
        ingrad_ref[i] = grad.astype(jnp.bfloat16)[:length]

    zone = ((z + 1 - 2 * (z % 2)) * 2 + x, shard)
    vec_steps = [
        remote(VS.at[k], VR.at[k], rss.at[3, k], rrs.at[3, k], who)
        for k, who in enumerate([sib, ypart, xpart, zone, zparts[1]])
    ]

    def vec(k):
        if k > 0:
            vec_steps[k - 1].wait_recv()
            VS[k] = VS[k - 1] + VR[k - 1]
        if k < 5:
            vec_steps[k].start()

    do_b(2)
    vec(0)
    do_f(1)
    do_end(0)
    vec(1)
    do_c(2)
    vec(2)
    do_d(2)
    vec(3)
    do_end(1)
    do_e(2)
    vec(4)
    do_f(2)
    vec(5)
    gvec_ref[...] = VS[5]
    do_end(2)

    for k in range(5):
        to_y[k].wait_send()
        to_sib[k].wait_send()
        forward[k].wait_send()
        vec_steps[k].wait_send()
    for n in range(3):
        step_a(n).wait_send()
        step_b(n).wait_send()
        for copy in steps_d(n) + steps_e(n):
            copy.wait_send()
        step_f(n).wait_send()


def finish(
    out_in, ingrad_in, sums, vectors, out_ref, ingrad_ref, gin_ref, gout_ref, gexp_ref, gred_ref, gbe_ref, *rest
):
    D = 384
    vector_refs, sem = rest[:8], rest[8]
    copies = [
        pltpu.make_async_copy(out_in, out_ref, sem.at[0]),
        pltpu.make_async_copy(ingrad_in, ingrad_ref, sem.at[1]),
    ]
    for copy in copies:
        copy.start()
    shard = lax.axis_index("shard")
    mine, expand = jnp.zeros((8, 96), jnp.float32), jnp.zeros((1, D), jnp.float32)
    for s in range(4):
        chosen = jnp.where(shard == s, 1.0, 0.0).astype(jnp.float32)
        mine = mine + chosen * vectors[0:8, s * 96 : s * 96 + 96]
        expand = expand + chosen * vectors[8 + s : 9 + s, :]
    for j in range(8):
        vector_refs[j][...] = mine[j : j + 1, :]
    gbe_ref[...] = expand
    gred_ref[...] = sums[0].astype(jnp.float32)
    for s in range(4):
        gexp_ref[:, s * D : s * D + D] = sums[1, s * 96 : s * 96 + 96, :].astype(jnp.float32)
    for s in range(3):
        gin_ref[:, s * D : s * D + D] = sums[2, s * 96 : s * 96 + 96, :].astype(jnp.float32)
    gout_ref[...] = sums[2, 288:384, :].astype(jnp.float32)
    for copy in copies:
        copy.wait()


def fused_body(
    images, counts, first_gain, first_shift, project_in, query_bias, value_bias, project_out, output_bias,
    second_gain, second_shift, expand_weight, expand_bias, reduce_weight, reduce_bias, cotangent,
):
    slots, length, width = images.shape
    rows = [first_gain, first_shift, query_bias, value_bias, output_bias, second_gain, second_shift, reduce_bias]
    pack = jnp.concatenate([jnp.stack(rows), expand_bias.reshape(4, 96)], axis=0)
    pack = jnp.pad(pack, ((0, 4), (0, 32)))
    f32, b16 = jnp.float32, jnp.bfloat16
    n = slots * ROWS
    vm = pl.BlockSpec(memory_space=pltpu.VMEM)
    scratch = [
        ((384, 1152), b16), ((384, 384), b16), ((384, 1536), b16), ((1536, 384), b16), ((64, 128), b16),
        ((16, 384), f32), ((8, 384), f32),
        ((n, 384), b16), ((n, 1152), b16), ((slots * HEADS, ROWS, ROWS), f32), ((n, 384), b16), ((n, 384), f32),
        ((n, 384), f32), ((n, 384), f32), ((n, 128), f32), ((n, 128), f32), ((n, 384), b16), ((n, 1536), b16),
        ((n, 1536), f32), ((n, 384), b16), ((n, 1536), b16), ((n, 384), f32), ((n, 384), b16), ((n, 384), b16),
        ((n, 1152), b16),
        ((3, 2, 2, 384, 384), b16), ((3, 2, 384, 384), b16), ((3, 384, 384), b16), ((3, 384, 384), b16),
        ((3, 384, 384), b16), ((3, 192, 384), b16), ((3, 3, 48, 384), b16), ((3, 384, 384), f32),
        ((6, 16, 384), f32), ((5, 16, 384), f32),
    ]
    outs = pl.pallas_call(
        mega,
        out_shape=[
            jax.ShapeDtypeStruct(images.shape, b16),
            jax.ShapeDtypeStruct(images.shape, b16),
            jax.ShapeDtypeStruct((3, 384, 384), b16),
            jax.ShapeDtypeStruct((16, 384), f32),
        ],
        in_specs=[vm, pl.BlockSpec(memory_space=pltpu.SMEM)] + [vm] * 6,
        out_specs=[vm] * 4,
        scratch_shapes=[pltpu.VMEM(shape, kind) for shape, kind in scratch]
        + [
            pltpu.SemaphoreType.DMA((3, 5)),
            pltpu.SemaphoreType.DMA((3, 5)),
            pltpu.SemaphoreType.DMA((4, 10)),
            pltpu.SemaphoreType.DMA((4, 10)),
        ],
        compiler_params=pltpu.CompilerParams(collective_id=0, has_side_effects=True, vmem_limit_bytes=60 * 2**20),
    )(images, counts, cotangent, pack, project_in, project_out, expand_weight, reduce_weight)
    anywhere = pl.BlockSpec(memory_space=pl.ANY)
    vector = jax.ShapeDtypeStruct((1, 96), f32)
    done = pl.pallas_call(
        finish,
        out_shape=[
            jax.ShapeDtypeStruct(images.shape, b16),
            jax.ShapeDtypeStruct(images.shape, b16),
            jax.ShapeDtypeStruct((96, 1152), f32),
            jax.ShapeDtypeStruct((96, 384), f32),
            jax.ShapeDtypeStruct((96, 1536), f32),
            jax.ShapeDtypeStruct((384, 384), f32),
            jax.ShapeDtypeStruct((1, 384), f32),
        ]
        + [vector] * 8,
        in_specs=[anywhere, anywhere, vm, vm],
        out_specs=[anywhere, anywhere] + [vm] * 13,
        scratch_shapes=[pltpu.SemaphoreType.DMA((2,))],
        compiler_params=pltpu.CompilerParams(vmem_limit_bytes=60 * 2**20),
    )(*outs)
    out, ingrad, gin, gout, gexp, gred, gbe = done[:7]
    v = [item.reshape(96) for item in done[7:]]
    return (
        out, ingrad, v[0], v[1], gin, v[2], v[3], gout, v[4], v[5], v[6], gexp, gbe.reshape(384), gred, v[7],
    )


def solution(mesh):
    fits = mesh.shape["replica"] == 8 and mesh.shape["shard"] == 4
    return jax.shard_map(
        fused_body if fits else body,
        mesh=mesh,
        in_specs=(
            P(("replica", "shard"), None, None),
            P(("replica", "shard")),
            P("shard"),
            P("shard"),
            P("shard", None),
            P("shard"),
            P("shard"),
            P("shard", None),
            P("shard"),
            P("shard"),
            P("shard"),
            P("shard", None),
            P("shard"),
            P("shard", None),
            P("shard"),
            P(("replica", "shard"), None, None),
        ),
        out_specs=(
            P(("replica", "shard"), None, None),
            P(("replica", "shard"), None, None),
            P("shard"),
            P("shard"),
            P("shard", None),
            P("shard"),
            P("shard"),
            P("shard", None),
            P("shard"),
            P("shard"),
            P("shard"),
            P("shard", None),
            P("shard"),
            P("shard", None),
            P("shard"),
        ),
        check_vma=False,
    )
```
